128 devices in a mesh: dp: 8 (over x, z_hi), ctx: 16 (over z_lo, y, core).
Axes of the slice: x: 4, y: 4, z: 4 (z_hi: 2, z_lo: 2; z = z_hi * 2 + z_lo), core: 2. Of those that a mesh axis runs over, the one named last changes fastest.
Arguments:
- events: bfloat16 [8, 4096, 512], P('dp', 'ctx'), may hold values from -6 to 6
- upstream: bfloat16 [8, 4096, 512], P('dp', 'ctx'), may hold values from -6 to 6
- lengths: int32 [8], P('dp'), may hold values from 1024 to 4096, as said below
- block_slots: int32 [32], replicated, may hold values from 0 to 31, as said below
- pattern: int32 [32, 3], replicated, may hold values from 0 to 31, as said below
- in_weight: bfloat16 [512, 2048], replicated, may hold values from -0.25 to 0.25
- out_weight: bfloat16 [512, 512], replicated, may hold values from -0.25 to 0.25
Outputs:
- encoded: bfloat16 [8, 4096, 512], P('dp', 'ctx')
- grad_events: bfloat16 [8, 4096, 512], P('dp', 'ctx')
- grad_in_weight: float32 [512, 2048], replicated
- grad_out_weight: float32 [512, 512], replicated
The draws below stay inside these ranges and needn't reach their ends.
Inputs may be any that keep to these rules, and one draw needn't show every extreme that they name: `lengths`: the first user's history fills all 4096 positions. A permutation: slot s of context device c holds history block block_slots[c * 2 + s]. `pattern`: every entry of row b is at most b, and row 0 is all zeros; entries may repeat; the query blocks held by one context device read at most 2 distinct key blocks held by any one other context device, and exactly 2 for some pair of devices.
All inputs are finite; a program needn't handle non-finite values.
Results may differ from the reference program's by a relative error of at most 0.012.
Values may be sent and summed in bfloat16 or wider, within the bound.
A program may use at most 128 MiB of HBM per device.

```python
import jax
import jax.numpy as jnp
from jax import lax

HEADS = 4
HD = 128
D = 512
BLK = 128
KSEL = 4
PAIR = 2
KEYS = 512
SEQ = 4096
BPD = 2
NB = 32
USERS = 8
N_CTX = 16


def shared_slots(key):
    return jax.random.permutation(key, NB).astype(jnp.int32)


def draw_lengths(key, part):
    key = jax.random.fold_in(key, 11)
    values = jax.random.randint(key, (USERS,), SEQ // 4, SEQ + 1)
    return values.at[0].set(SEQ).astype(jnp.int32)


def draw_block_slots(key, part):
    return shared_slots(key)


def draw_pattern(key, part):
    slots = shared_slots(key)
    key = jax.random.fold_in(key, 23)
    place = jnp.argsort(slots).astype(jnp.int32)
    owner = (place // BPD).astype(jnp.int32)
    raw = jax.random.randint(key, (NB, KSEL - 1, NB), 0, 1 << 15).astype(jnp.int32)
    marks = jnp.arange(NB, dtype=jnp.int32)
    final = NB - 1

    def step(counts, block):
        mine = owner[block]
        earlier = marks < block
        foreign = owner != mine
        is_last = block == final
        picks = []
        first = jnp.int32(0)
        for slot in range(KSEL - 1):
            room = counts[mine][owner] < PAIR
            allowed = earlier & (jnp.logical_not(foreign) | room)
            if slot == 0:
                allowed = jnp.where(is_last, allowed & foreign, allowed)
            elif slot == 1:
                allowed = jnp.where(is_last, allowed & (owner == owner[first]) & (marks != first), allowed)
            else:
                allowed = jnp.where(is_last, marks == block, allowed)
            score = jnp.where(allowed, raw[block, slot] * NB + marks, -1)
            best = jnp.argmax(score).astype(jnp.int32)
            chosen = jnp.where(score[best] >= 0, best, block).astype(jnp.int32)
            added = jnp.where(owner[chosen] != mine, 1, 0).astype(jnp.int32)
            counts = counts.at[mine, owner[chosen]].add(added)
            if slot == 0:
                first = chosen
            picks.append(chosen)
        return (counts, jnp.stack(picks))
    start = jnp.zeros((N_CTX, N_CTX), jnp.int32)
    _, table = lax.scan(step, start, marks[::-1])
    return table[::-1].astype(jnp.int32)


def block_scale(own_key, dims, pieces, low, top_value):
    level = 1.0
    for dim, blocks in pieces:
        heights = jax.random.uniform(jax.random.fold_in(jax.random.fold_in(own_key, 6), dim), (blocks,), jnp.float32, low / len(pieces), top_value / len(pieces))
        level = level * jnp.repeat(jnp.exp(heights), dims[dim] // blocks).reshape((-1,) + (1,) * (len(dims) - 1 - dim))
    return level


def normal_values(rng, extent, scale, reach, pieces=(), kind=jnp.bfloat16):
    array = scale * jax.random.normal(rng, extent, jnp.float32)
    if pieces:
        array = array * block_scale(rng, extent, pieces, -0.22, 0.18)
    return jnp.clip(array, -reach, reach).astype(kind)


def setup_inputs(seed: int = 0) -> dict:
    key_of = jax.random.split(jax.random.key(seed), 8)
    events = normal_values(key_of[0], (USERS, SEQ, D), 1.0, 6.0, ((0, 8), (1, 16)))
    upstream = normal_values(key_of[1], (USERS, SEQ, D), 1.0, 6.0, ((0, 8), (1, 16)))
    lengths = draw_lengths(jax.random.fold_in(key_of[7], 71), 0)
    block_slots = draw_block_slots(jax.random.fold_in(key_of[7], 71), 0)
    pattern = draw_pattern(jax.random.fold_in(key_of[7], 71), 0)
    in_weight = normal_values(key_of[5], (D, 4 * D), D ** -0.5, 0.25)
    out_weight = normal_values(key_of[6], (D, D), D ** -0.5, 0.25)
    return dict(events=events, upstream=upstream, lengths=lengths, block_slots=block_slots, pattern=pattern, in_weight=in_weight, out_weight=out_weight)


eps_norm = 1e-05

def silu_slope(value):
    sigma = jax.nn.sigmoid(value)
    return sigma * (1.0 + value * (1.0 - sigma))

def norm_rows(value):
    centre = value - lax.optimization_barrier(jnp.mean(value, axis=-1, keepdims=True))
    inverse = lax.rsqrt(lax.optimization_barrier(jnp.mean(centre * centre, axis=-1, keepdims=True)) + eps_norm)
    return (centre * inverse, inverse)

def norm_back(grad_hat, normal, inverse):
    return inverse * (grad_hat - lax.optimization_barrier(jnp.mean(grad_hat, -1, keepdims=True)) - normal * lax.optimization_barrier(jnp.mean(grad_hat * normal, -1, keepdims=True)))

def block_plan(block_slots, pattern, length, query_slots, blocks):
    store = jnp.arange(blocks, dtype=jnp.int32)
    slot_of = lax.optimization_barrier(jnp.sum(store[None, :] * (block_slots[None, :] == store[:, None]).astype(jnp.int32), axis=1)).astype(jnp.int32)
    global_q = block_slots[query_slots]
    listed = jnp.concatenate([global_q[:, None], pattern[global_q]], axis=1).astype(jnp.int32)
    same = listed[:, :, None] == listed[:, None, :]
    earlier = jnp.arange(KSEL)[None, :] < jnp.arange(KSEL)[:, None]
    fresh = jnp.logical_not(jnp.any(same & earlier[None], axis=2))
    offsets = jnp.arange(BLK, dtype=jnp.int32)
    q_pos = global_q[:, None] * BLK + offsets[None, :]
    k_pos = (listed[:, :, None] * BLK + offsets[None, None, :]).reshape(query_slots.shape[0], KSEL * BLK)
    k_live = jnp.repeat(fresh, BLK, axis=1) & (k_pos < length)
    mask = k_live[:, None, :] & (k_pos[:, None, :] <= q_pos[:, :, None]) & (q_pos < length)[:, :, None]
    return (slot_of[listed], mask.astype(jnp.float32))

def one_user(history, upstream, length, block_slots, pattern, in_weight, out_weight):
    f32 = jnp.float32
    bf16 = jnp.bfloat16
    scale = HD ** (-0.5)
    hat_in, inv_in = norm_rows(history.astype(f32))
    normed = hat_in.astype(bf16)
    preact = jnp.dot(normed, in_weight, preferred_element_type=f32)
    active = jax.nn.silu(preact).astype(bf16)
    feat_u = active[:, :D]
    feat_v = active[:, D:2 * D]
    feat_q = active[:, 2 * D:3 * D]
    feat_k = active[:, 3 * D:]
    key_store, mask = block_plan(block_slots, pattern, length, jnp.arange(NB, dtype=jnp.int32), NB)
    k_sel = feat_k.reshape(NB, BLK, D)[key_store].reshape(NB, KEYS, HEADS, HD).astype(f32)
    v_sel = feat_v.reshape(NB, BLK, D)[key_store].reshape(NB, KEYS, HEADS, HD).astype(f32)
    q_blk = feat_q.reshape(NB, BLK, HEADS, HD).astype(f32)
    scores = jnp.einsum('bihd,bjhd->bhij', q_blk, k_sel) * scale
    weights = (jax.nn.silu(scores) * mask[:, None]).astype(bf16)
    mixed = jnp.einsum('bhij,bjhd->bihd', weights.astype(f32), v_sel).reshape(SEQ, D)
    hat_mix, inv_mix = norm_rows(mixed)
    gated = (hat_mix * feat_u.astype(f32)).astype(bf16)
    encoded = (history.astype(f32) + jnp.dot(gated, out_weight, preferred_element_type=f32)).astype(bf16)
    grad_gated = jnp.dot(upstream, out_weight.T, preferred_element_type=f32)
    grad_out = jnp.dot(gated.T, upstream, preferred_element_type=f32)
    grad_u = grad_gated * hat_mix
    grad_mixed = norm_back(grad_gated * feat_u.astype(f32), hat_mix, inv_mix).astype(bf16)
    grad_mh = grad_mixed.reshape(NB, BLK, HEADS, HD).astype(f32)
    grad_weights = jnp.einsum('bihd,bjhd->bhij', grad_mh, v_sel)
    grad_scores = (grad_weights * silu_slope(scores) * mask[:, None] * scale).astype(bf16).astype(f32)
    grad_q = jnp.einsum('bhij,bjhd->bihd', grad_scores, k_sel).reshape(SEQ, D)
    grad_k_sel = jnp.einsum('bhij,bihd->bjhd', grad_scores, q_blk).reshape(NB, KSEL, BLK, D)
    grad_v_sel = jnp.einsum('bhij,bihd->bjhd', weights.astype(f32), grad_mh).reshape(NB, KSEL, BLK, D)

    def device_term(totals, device):
        index = lax.dynamic_slice_in_dim(key_store, device * BPD, BPD, 0).reshape(-1)
        part_k = lax.dynamic_slice_in_dim(grad_k_sel, device * BPD, BPD, 0).reshape(BPD * KSEL, BLK, D)
        part_v = lax.dynamic_slice_in_dim(grad_v_sel, device * BPD, BPD, 0).reshape(BPD * KSEL, BLK, D)
        sum_k = jnp.zeros((NB, BLK, D), f32).at[index].add(part_k)
        sum_v = jnp.zeros((NB, BLK, D), f32).at[index].add(part_v)
        sum_k = lax.optimization_barrier(sum_k.astype(bf16)).astype(f32)
        sum_v = lax.optimization_barrier(sum_v.astype(bf16)).astype(f32)
        return ((totals[0] + sum_k, totals[1] + sum_v), None)
    zeros = jnp.zeros((NB, BLK, D), f32)
    totals, _ = lax.scan(device_term, (zeros, zeros), jnp.arange(N_CTX, dtype=jnp.int32))
    grad_k = totals[0].reshape(SEQ, D)
    grad_v = totals[1].reshape(SEQ, D)
    grad_act = jnp.concatenate([grad_u, grad_v, grad_q, grad_k], axis=1)
    grad_pre = (grad_act * silu_slope(preact)).astype(bf16)
    grad_in = jnp.dot(normed.T, grad_pre, preferred_element_type=f32)
    grad_normed = jnp.dot(grad_pre, in_weight.T, preferred_element_type=f32)
    grad_events = (upstream.astype(f32) + norm_back(grad_normed, hat_in, inv_in)).astype(bf16)
    return (encoded, grad_events, grad_in, grad_out)

def reference(events, upstream, lengths, block_slots, pattern, in_weight, out_weight):
    outputs = []
    grads = []
    grad_in = jnp.zeros((D, 4 * D), jnp.float32)
    grad_out = jnp.zeros((D, D), jnp.float32)
    for user in range(USERS):
        encoded, grad_events, term_in, term_out = one_user(events[user], upstream[user], lengths[user], block_slots, pattern, in_weight, out_weight)
        outputs.append(encoded)
        grads.append(grad_events)
        grad_in = grad_in + term_in
        grad_out = grad_out + term_out
    return (jnp.stack(outputs), jnp.stack(grads), grad_in, grad_out)
```

```python
import functools

import jax
import jax.numpy as jnp
from jax import lax
from jax.experimental import pallas as pl
from jax.experimental.pallas import tpu as pltpu
from jax.sharding import PartitionSpec as P

HEADS = 4
HD = 128
BLK = 128
D = 512
EPS = 1e-05
SCALE = HD ** (-0.5)
MESH = pl.DeviceIdType.MESH
F32 = jnp.float32
BF16 = jnp.bfloat16
FAR = 1 << 20
G_OUT, G_U, G_Q, G_V, G_K = 0, 512, 1024, 1536, 2048
GCOLS = 2560
N_SEM = 96


def dot(a, b):
    return jnp.dot(a, b, preferred_element_type=F32)


def dot_nt(a, b):
    return lax.dot_general(a, b, (((1,), (1,)), ((), ())), preferred_element_type=F32)


def dot_tn(a, b):
    return lax.dot_general(a, b, (((0,), (0,)), ((), ())), preferred_element_type=F32)


def sigmoid(z):
    return 0.5 + 0.5 * jnp.tanh(0.5 * z)


def norm_rows(z):
    centre = z - jnp.mean(z, axis=-1, keepdims=True)
    inverse = lax.rsqrt(jnp.mean(centre * centre, axis=-1, keepdims=True) + EPS)
    return centre * inverse, inverse


def norm_back(grad, hat, inverse):
    return inverse * (
        grad
        - jnp.mean(grad, axis=-1, keepdims=True)
        - hat * jnp.mean(grad * hat, axis=-1, keepdims=True)
    )


class Net:
    def __init__(self, send_sems, recv_sems):
        self.send_sems, self.recv_sems = send_sems, recv_sems
        self.copies = []

    def send(self, src, dst, device):
        at = len(self.copies)
        copy = pltpu.make_async_remote_copy(
            src_ref=src,
            dst_ref=dst,
            send_sem=self.send_sems.at[at],
            recv_sem=self.recv_sems.at[at],
            device_id=device,
            device_id_type=MESH,
        )
        copy.start()
        self.copies.append((copy, device))
        return at

    def landed(self, at, ref):
        pltpu.make_async_remote_copy(
            src_ref=ref,
            dst_ref=ref,
            send_sem=self.send_sems.at[at],
            recv_sem=self.recv_sems.at[at],
            device_id=self.copies[at][1],
            device_id_type=MESH,
        ).wait_recv()

    def drain(self):
        for copy, _ in self.copies:
            copy.wait_send()


def layer_kernel(
    slots_ref, pattern_ref, length_ref, events, upstream, w_hbm, wo_hbm,
    encoded, grad_events, gw,
    w, wo, gx, normed, own_normed, hat_in, inv_in,
    u_act, u_slope, q_act, q_slope, k_act, k_slope, v_act, v_slope,
    grad_gated, limit_mask, weights, slope, mixed, grad_mixed, grad_q,
    dv, dk, own_grad, compact,
    to_sib, from_sib, sum_y, sum_z, r_z2, r_ya, r_yb, r_h, r_p, r_m, r_z0,
    gp, g_sib, g_x, g_z, g_y, g_zs,
    w_sems, send_sems, recv_sems,
):
    dp = lax.axis_index("dp")
    ctx = lax.axis_index("ctx")
    x, zh = dp // 2, dp % 2
    zl, y, core = ctx // 8, (ctx // 2) % 4, ctx % 2
    z = zh * 2 + zl

    def dev(x, y, z, core):
        return {"dp": x * 2 + z // 2, "ctx": ((z % 2) * 4 + y) * 2 + core}

    def rot(v, by):
        return lax.rem(v + by, 4)

    sib = dev(x, y, z, 1 - core)
    yp, ym, y2 = (dev(x, rot(y, i), z, core) for i in (1, 3, 2))
    zp = dev(x, y, zh * 2 + 1 - zl, core)
    ring_x = [dev(rot(x, i), y, z, core) for i in range(4)]
    ring_y = [dev(x, rot(y, i), z, core) for i in range(4)]
    ring_z = [dev(x, y, rot(z, i), core) for i in range(4)]

    w_copy = pltpu.make_async_copy(w_hbm, w, w_sems.at[0])
    wo_copy = pltpu.make_async_copy(wo_hbm, wo, w_sems.at[1])
    w_copy.start()
    wo_copy.start()

    barrier = pltpu.get_barrier_semaphore()
    partners = [sib] + ring_x[1:] + ring_y[1:] + ring_z[1:]
    for partner in partners:
        pl.semaphore_signal(barrier, inc=1, device_id=partner, device_id_type=MESH)

    net = Net(send_sems, recv_sems)

    def shard(dz, dy, side):
        zz = zl if dz == 0 else 1 - zl
        kk = core if side == 0 else 1 - core
        return ((zz * 4 + rot(y, dy)) * 2 + kk) * 2

    def rows(dz, dy, side=0, half=None):
        base = shard(dz, dy, side)
        if half is None:
            return gx.at[pl.ds(base, 2)]
        return gx.at[base + half]

    for half in range(2):
        gx[shard(0, 0, 0) + half] = events[half * 128 : half * 128 + 128, :]
    pl.semaphore_wait(barrier, len(partners))

    def forward(ref, device):
        return net.send(ref, ref, device)

    a_yp0 = forward(rows(0, 0, 0, 0), yp)
    a_ym0 = forward(rows(0, 0, 0, 1), ym)
    a_z0 = forward(rows(0, 0, 0, 0), zp)
    a_sib = forward(rows(0, 0), sib)
    a_yp1 = forward(rows(0, 0, 0, 1), yp)
    a_ym1 = forward(rows(0, 0, 0, 0), ym)
    a_z1 = forward(rows(0, 0, 0, 1), zp)

    hat, inv = norm_rows(events[...].astype(F32))
    hat_in[...] = hat
    inv_in[...] = inv
    own = hat.astype(BF16)
    own_normed[...] = own
    for b in range(2):
        normed[b * 512 : b * 512 + 128, :] = own[b * 128 : b * 128 + 128]
    w_copy.wait()
    wo_copy.wait()

    def activate(pre):
        sig = sigmoid(pre)
        act = pre * sig
        return act.astype(BF16), sig + act * (1.0 - sig)

    for h in range(4):
        act, sl = activate(dot(own_normed[...], w[:, h * 128 : h * 128 + 128]))
        u_act[h] = act
        u_slope[h] = sl
        act, sl = activate(dot(own_normed[...], w[:, 1024 + h * 128 : 1152 + h * 128]))
        q_act[h] = act
        q_slope[h] = sl

    net.landed(a_yp0, rows(0, 3, 0, 0))
    r_yp = forward(rows(0, 3, 0, 0), yp)
    net.landed(a_ym0, rows(0, 1, 0, 1))
    r_ym = forward(rows(0, 1, 0, 1), ym)
    net.landed(a_z0, rows(1, 0, 0, 0))
    f_yp0 = forward(rows(1, 0, 0, 0), yp)
    f_ym0 = forward(rows(1, 0, 0, 0), ym)

    for h in range(4):
        grad_gated[h] = dot_nt(upstream[...], wo[h * 128 : h * 128 + 128, :])

    def project(lo, n):
        for h in range(4):
            act, sl = activate(dot(normed[pl.ds(lo, n), :], w[:, 512 + h * 128 : 640 + h * 128]))
            v_act[h, pl.ds(lo, n), :] = act
            v_slope[h, pl.ds(lo, n), :] = sl
            act, sl = activate(dot(normed[pl.ds(lo, n), :], w[:, 1536 + h * 128 : 1664 + h * 128]))
            k_act[h, pl.ds(lo, n), :] = act
            k_slope[h, pl.ds(lo, n), :] = sl

    net.landed(a_yp1, rows(0, 3, 0, 1))
    d1 = forward(rows(0, 3), sib)
    net.landed(a_ym1, rows(0, 1, 0, 0))
    d2 = forward(rows(0, 1), sib)
    net.landed(a_z1, rows(1, 0, 0, 1))
    f_yp1 = forward(rows(1, 0, 0, 1), yp)
    f_ym1 = forward(rows(1, 0, 0, 1), ym)
    d3 = forward(rows(1, 0), sib)
    project(0, 128)
    project(512, 128)
    net.landed(r_yp, rows(0, 2, 0, 0))
    z2_0 = forward(rows(0, 2, 0, 0), zp)
    net.landed(r_ym, rows(0, 2, 0, 1))
    z2_1 = forward(rows(0, 2, 0, 1), zp)
    d4 = forward(rows(0, 2), sib)

    length = length_ref[0]
    listed, at_slot, fresh = [], [], []
    for b in range(2):
        mine = slots_ref[2 * ctx + b]
        picks = [mine] + [pattern_ref[mine, t] for t in range(3)]
        listed.append(picks)
        news = [None]
        for t in range(1, 4):
            new = picks[t] != picks[0]
            for s in range(1, t):
                new = jnp.logical_and(new, picks[t] != picks[s])
            news.append(new)
        fresh.append(news)
    found = [[jnp.int32(0)] * 4 for _ in range(2)]
    for s in range(32):
        block = slots_ref[s]
        for b in range(2):
            for t in range(1, 4):
                found[b][t] = jnp.where(block == listed[b][t], s, found[b][t])

    for b in range(2):
        q_pos = listed[b][0] * 128 + lax.broadcasted_iota(jnp.int32, (128, 128), 0)
        top = jnp.where(q_pos < length, q_pos, -1)
        lane = lax.broadcasted_iota(jnp.int32, (128, 128), 1)
        for t in range(4):
            start = listed[b][t] * 128
            if t:
                start = jnp.where(fresh[b][t], start, FAR)
            limit_mask[b, :, t * 128 : t * 128 + 128] = (start + lane <= top).astype(F32)

    net.landed(f_yp0, rows(1, 3, 0, 0))
    net.landed(f_yp1, rows(1, 3, 0, 1))
    d5 = forward(rows(1, 3), sib)
    net.landed(f_ym0, rows(1, 1, 0, 0))
    net.landed(f_ym1, rows(1, 1, 0, 1))
    d6 = forward(rows(1, 1), sib)
    net.landed(z2_0, rows(1, 2, 0, 0))
    net.landed(z2_1, rows(1, 2, 0, 1))
    d7 = forward(rows(1, 2), sib)
    for at, (dz, dy) in zip(
        (a_sib, d1, d2, d3, d4, d5, d6, d7),
        ((0, 0), (0, 3), (0, 1), (1, 0), (0, 2), (1, 3), (1, 1), (1, 2)),
    ):
        net.landed(at, rows(dz, dy, 1))

    for b in range(2):
        for t in range(1, 4):
            block = gx[found[b][t]]
            normed[b * 512 + t * 128 : b * 512 + t * 128 + 128, :] = norm_rows(block.astype(F32))[
                0
            ].astype(BF16)
    project(128, 384)
    project(640, 384)

    def forward_head(i, carry):
        b, h = i // 4, i % 4
        q = q_act[h, pl.ds(pl.multiple_of(b * 128, 128), 128), :]
        for t in range(4):
            lo = pl.multiple_of(b * 512 + t * 128, 128)
            s = dot_nt(q, k_act[h, pl.ds(lo, 128), :]) * SCALE
            mask = limit_mask[b, :, t * 128 : t * 128 + 128]
            sig = sigmoid(s)
            act = s * sig
            weights[i, :, t * 128 : t * 128 + 128] = (act * mask).astype(BF16)
            slope[i, :, t * 128 : t * 128 + 128] = (sig + act * (1.0 - sig)) * (mask * SCALE)
        mixed[h, pl.ds(pl.multiple_of(b * 128, 128), 128), :] = dot(
            weights[i], v_act[h, pl.ds(pl.multiple_of(b * 512, 512), 512), :]
        )
        return carry

    lax.fori_loop(0, 8, forward_head, 0)

    def across(parts):
        return sum(jnp.sum(part, axis=-1, keepdims=True) for part in parts) * (1.0 / D)

    parts = [mixed[h] for h in range(4)]
    mean = across(parts)
    parts = [part - mean for part in parts]
    inv_mix = lax.rsqrt(across([part * part for part in parts]) + EPS)
    hats = [part * inv_mix for part in parts]
    us = [u_act[h].astype(F32) for h in range(4)]
    gated = jnp.concatenate([(hats[h] * us[h]).astype(BF16) for h in range(4)], axis=1)
    encoded[...] = (events[...].astype(F32) + dot(gated, wo[...])).astype(BF16)
    gp[:, G_OUT : G_OUT + 512] = dot_tn(gated, upstream[...]).astype(BF16)
    ggs = [grad_gated[h] for h in range(4)]
    du = jnp.concatenate([(ggs[h] * hats[h] * u_slope[h]).astype(BF16) for h in range(4)], axis=1)
    gp[:, G_U : G_U + 512] = dot_tn(own_normed[...], du).astype(BF16)
    own_grad[...] = dot_nt(du, w[:, 0:512])
    ts = [ggs[h] * us[h] for h in range(4)]
    mean_t = across(ts)
    mean_th = across([ts[h] * hats[h] for h in range(4)])
    for h in range(4):
        grad_mixed[h] = (inv_mix * (ts[h] - mean_t - hats[h] * mean_th)).astype(BF16)

    def backward_head(i, carry):
        b, h = i // 4, i % 4
        q_rows = pl.ds(pl.multiple_of(b * 128, 128), 128)
        k_rows = pl.ds(pl.multiple_of(b * 512, 512), 512)
        gm = grad_mixed[h, q_rows, :]
        q = q_act[h, q_rows, :]
        gs = (dot_nt(gm, v_act[h, k_rows, :]) * slope[i]).astype(BF16)
        grad_q[h, q_rows, :] = dot(gs, k_act[h, k_rows, :])
        dk[h, k_rows, :] = (dot_tn(gs, q) * k_slope[h, k_rows, :]).astype(BF16)
        dv[h, k_rows, :] = (dot_tn(weights[i], gm) * v_slope[h, k_rows, :]).astype(BF16)
        return carry

    lax.fori_loop(0, 8, backward_head, 0)

    dv_all = jnp.concatenate([dv[h] for h in range(4)], axis=1)
    dk_all = jnp.concatenate([dk[h] for h in range(4)], axis=1)
    back = dot_nt(dv_all, w[:, 512:1024]) + dot_nt(dk_all, w[:, 1536:2048])
    for b in range(2):
        for t in range(1, 4):
            lo = b * 512 + t * 128
            compact[b * 3 + t - 1] = back[lo : lo + 128].astype(BF16)
        own_grad[b * 128 : b * 128 + 128, :] += back[b * 512 : b * 512 + 128]
    compact[6] = jnp.zeros((128, 512), BF16)

    def pieces(dz, dy, side):
        zz = zl if dz == 0 else 1 - zl
        kk = core if side == 0 else 1 - core
        base = ((zz * 4 + rot(y, dy)) * 2 + kk) * 2
        out = []
        for i in range(2):
            total = []
            for b in range(2):
                at = jnp.int32(6)
                for t in range(1, 4):
                    hit = jnp.logical_and(found[b][t] == base + i, fresh[b][t])
                    at = jnp.where(hit, b * 3 + t - 1, at)
                total.append(compact[at])
            out.append(total)
        return out

    order = ((1, 2), (1, 1), (1, 3), (0, 2), (1, 0), (0, 1), (0, 3), (0, 0))
    sib_at = {}
    for dz, dy in order:
        j = dz * 4 + dy
        for i, (p0, p1) in enumerate(pieces(dz, dy, 1)):
            to_sib[j, i * 128 : i * 128 + 128, :] = p0 + p1
        sib_at[j] = net.send(to_sib.at[j], from_sib.at[j], sib)

    def chip_sum(dz, dy, half):
        p0, p1 = pieces(dz, dy, 0)[half]
        j = dz * 4 + dy
        return (
            p0.astype(F32) + p1.astype(F32)
            + from_sib[j, half * 128 : half * 128 + 128, :].astype(F32)
        )

    def half_of(ref, half):
        return ref[half * 128 : half * 128 + 128, :].astype(F32)

    def outgoing(buf, dz, dy, extra=()):
        for half in range(2):
            total = chip_sum(dz, dy, half)
            for ref in extra:
                total = total + half_of(ref, half)
            buf[half * 128 : half * 128 + 128, :] = total.astype(BF16)

    def sib_landed(dz, dy):
        j = dz * 4 + dy
        net.landed(sib_at[j], from_sib.at[j])

    sib_landed(1, 2)
    outgoing(sum_z.at[0], 1, 2)
    s_z2 = net.send(sum_z.at[0], r_z2, zp)
    sib_landed(1, 1)
    outgoing(sum_y.at[0], 1, 1)
    s_ya = net.send(sum_y.at[0], r_ya, yp)
    sib_landed(1, 3)
    outgoing(sum_y.at[1], 1, 3)
    s_yb = net.send(sum_y.at[1], r_yb, ym)

    gp[:, G_V : G_V + 512] = dot_tn(normed[...], dv_all).astype(BF16)
    gp[:, G_K : G_K + 512] = dot_tn(normed[...], dk_all).astype(BF16)
    dq = jnp.concatenate([(grad_q[h] * q_slope[h]).astype(BF16) for h in range(4)], axis=1)
    gp[:, G_Q : G_Q + 512] = dot_tn(own_normed[...], dq).astype(BF16)
    own_grad[...] += dot_nt(dq, w[:, 1024:1536])

    half_cols = GCOLS // 2
    mine = pl.ds(pl.multiple_of(core * half_cols, half_cols), half_cols)
    other = pl.ds(pl.multiple_of((1 - core) * half_cols, half_cols), half_cols)
    s_g = net.send(gp.at[:, other], g_sib, sib)

    sib_landed(0, 2)
    net.landed(s_z2, r_z2)
    outgoing(sum_y.at[2], 0, 2, (r_z2,))
    s_h0 = net.send(sum_y.at[2, pl.ds(0, 128)], r_h.at[0], yp)
    s_h1 = net.send(sum_y.at[2, pl.ds(128, 128)], r_h.at[1], ym)

    net.landed(s_g, g_sib)
    for r in range(4):
        part = pl.ds(r * 128, 128)
        g_sib[part, :] = (gp[part, mine].astype(F32) + g_sib[part, :].astype(F32)).astype(BF16)

    def span(v, n):
        return pl.ds(pl.multiple_of(v * n, n), n)

    x_at = [
        net.send(g_sib.at[span(rot(x, i), 128)], g_x.at[i], ring_x[i]) for i in (1, 3, 2)
    ]

    sib_landed(1, 0)
    net.landed(s_ya, r_ya)
    net.landed(s_yb, r_yb)
    outgoing(sum_z.at[1], 1, 0, (r_ya, r_yb))
    s_z0 = net.send(sum_z.at[1], r_z0, zp)

    sib_landed(0, 1)
    sib_landed(0, 3)
    net.landed(s_h0, r_h.at[0])
    net.landed(s_h1, r_h.at[1])
    sum_y[3, 0:128, :] = (chip_sum(0, 1, 0) + r_h[0].astype(F32)).astype(BF16)
    sum_y[3, 128:256, :] = chip_sum(0, 1, 1).astype(BF16)
    s_p = net.send(sum_y.at[3], r_p, yp)
    sum_y[4, 0:128, :] = chip_sum(0, 3, 0).astype(BF16)
    sum_y[4, 128:256, :] = (chip_sum(0, 3, 1) + r_h[1].astype(F32)).astype(BF16)
    s_m = net.send(sum_y.at[4], r_m, ym)

    for at, i in zip(x_at, (1, 3, 2)):
        net.landed(at, g_x.at[i])
    g_x[0] = (
        g_sib[span(x, 128), :].astype(F32)
        + g_x[1].astype(F32) + g_x[2].astype(F32) + g_x[3].astype(F32)
    ).astype(BF16)
    z_at = [
        net.send(g_x.at[0, span(rot(z, i), 32)], g_z.at[i], ring_z[i]) for i in (1, 3, 2)
    ]

    sib_landed(0, 0)
    net.landed(s_p, r_p)
    net.landed(s_m, r_m)
    net.landed(s_z0, r_z0)
    for half in range(2):
        part = pl.ds(half * 128, 128)
        total = own_grad[part, :] + chip_sum(0, 0, half)
        for ref in (r_p, r_m, r_z0):
            total = total + half_of(ref, half)
        grad_events[part, :] = (
            upstream[part, :].astype(F32) + norm_back(total, hat_in[part, :], inv_in[part, :])
        ).astype(BF16)

    for at, i in zip(z_at, (1, 3, 2)):
        net.landed(at, g_z.at[i])
    g_zs[...] = (
        g_x[0, span(z, 32), :].astype(F32)
        + g_z[1].astype(F32) + g_z[2].astype(F32) + g_z[3].astype(F32)
    ).astype(BF16)
    g_y[y] = g_zs[...]
    y_at = [net.send(g_zs, g_y.at[y], ring_y[i]) for i in (1, 3, 2)]
    for at, i in zip(y_at, (3, 1, 2)):
        net.landed(at, g_y.at[rot(y, i)])
    final = (
        g_y[0].astype(F32) + g_y[1].astype(F32) + g_y[2].astype(F32) + g_y[3].astype(F32)
    ).astype(BF16)

    def block(vx, vz=None):
        if vz is None:
            return pl.ds(pl.multiple_of(vx * 128, 128), 128)
        return pl.ds(pl.multiple_of(vx * 128 + vz * 32, 32), 32)

    gw[block(x, z), mine] = final
    here = gw.at[block(x, z), mine]
    z_at = [net.send(here, here, ring_z[i]) for i in (1, 3, 2)]
    for at, i in zip(z_at, (3, 1, 2)):
        net.landed(at, gw.at[block(x, rot(z, i)), mine])
    here = gw.at[block(x), mine]
    x_at = [net.send(here, here, ring_x[i]) for i in (1, 3, 2)]
    sib_back = [net.send(here, here, sib)]
    for at, i in zip(x_at, (3, 1, 2)):
        there = gw.at[block(rot(x, i)), mine]
        net.landed(at, there)
        sib_back.append(net.send(there, there, sib))
    for at, i in zip(sib_back, (0, 3, 1, 2)):
        net.landed(at, gw.at[block(rot(x, i)), other])
    net.drain()


def local(events, upstream, lengths, block_slots, pattern, in_weight, out_weight):
    vmem = pl.BlockSpec(memory_space=pltpu.VMEM)
    smem = pl.BlockSpec(memory_space=pltpu.SMEM)
    hbm = pl.BlockSpec(memory_space=pl.ANY)
    v = pltpu.VMEM
    half = GCOLS // 2
    scratch = [
        v((512, 2048), BF16), v((512, 512), BF16), v((32, 128, 512), BF16),
        v((1024, 512), BF16), v((256, 512), BF16), v((256, 512), F32), v((256, 1), F32),
        v((4, 256, 128), BF16), v((4, 256, 128), F32),
        v((4, 256, 128), BF16), v((4, 256, 128), F32),
        v((4, 1024, 128), BF16), v((4, 1024, 128), F32),
        v((4, 1024, 128), BF16), v((4, 1024, 128), F32),
        v((4, 256, 128), F32), v((2, 128, 512), F32), v((8, 128, 512), BF16),
        v((8, 128, 512), F32), v((4, 256, 128), F32), v((4, 256, 128), BF16),
        v((4, 256, 128), F32),
        v((4, 1024, 128), BF16), v((4, 1024, 128), BF16), v((256, 512), F32),
        v((7, 128, 512), BF16),
        v((8, 256, 512), BF16), v((8, 256, 512), BF16), v((5, 256, 512), BF16),
        v((2, 256, 512), BF16),
        v((256, 512), BF16), v((256, 512), BF16), v((256, 512), BF16), v((2, 128, 512), BF16),
        v((256, 512), BF16), v((256, 512), BF16), v((256, 512), BF16),
        v((512, GCOLS), BF16), v((512, half), BF16), v((4, 128, half), BF16), v((4, 32, half), BF16),
        v((4, 32, half), BF16), v((32, half), BF16),
        pltpu.SemaphoreType.DMA((2,)),
        pltpu.SemaphoreType.DMA((N_SEM,)),
        pltpu.SemaphoreType.DMA((N_SEM,)),
    ]
    encoded, grad_events, gw = pl.pallas_call(
        layer_kernel,
        out_shape=(
            jax.ShapeDtypeStruct((256, D), BF16),
            jax.ShapeDtypeStruct((256, D), BF16),
            jax.ShapeDtypeStruct((512, GCOLS), BF16),
        ),
        in_specs=[smem, smem, smem, vmem, vmem, hbm, hbm],
        out_specs=(vmem, vmem, vmem),
        scratch_shapes=scratch,
        compiler_params=pltpu.CompilerParams(
            collective_id=0, has_side_effects=True, vmem_limit_bytes=56 * 2**20
        ),
        name="layer",
    )(block_slots, pattern, lengths, events[0], upstream[0], in_weight, out_weight)
    grad_in = jnp.concatenate(
        [gw[:, g : g + 512] for g in (G_U, G_V, G_Q, G_K)], axis=1
    ).astype(F32)
    grad_out = gw[:, G_OUT : G_OUT + 512].astype(F32)
    return encoded[None], grad_events[None], grad_in, grad_out


def solution(mesh):
    return jax.shard_map(
        local,
        mesh=mesh,
        in_specs=(P("dp", "ctx", None), P("dp", "ctx", None), P("dp"), P(), P(), P(), P()),
        out_specs=(P("dp", "ctx", None), P("dp", "ctx", None), P(), P()),
        check_vma=False,
    )
```

```python
import functools

import jax
import jax.numpy as jnp
from jax import lax
from jax.experimental import pallas as pl
from jax.experimental.pallas import tpu as pltpu
from jax.sharding import PartitionSpec as P

HEADS = 4
HD = 128
BLK = 128
D = 512
EPS = 1e-05
SCALE = HD ** (-0.5)
MESH = pl.DeviceIdType.MESH
F32 = jnp.float32
BF16 = jnp.bfloat16
FAR = 1 << 20
G_OUT, G_U, G_V, G_Q, G_K = 0, 512, 1024, 1536, 2048
GCOLS = 2560
N_SEM = 176
PARTS = (
    ("ou", G_OUT, 1024, ("y", "x", "z")),
    ("v", G_V, 512, ("x", "z", "y")),
    ("k", G_K, 512, ("x", "y", "z")),
    ("q", G_Q, 512, ("z", "x", "y")),
)
SCHEDULE = (
    "ou", "value_heads", "score_heads", "ou", "weight_k", "weight_q", "weight_v", "v", "q",
    "k", "back_rows", "d2d_a", "q", "k", "v", "far_z", "far_y", "d2d_b",
    "ou", "q", "k", "own_rows", "encode", "near_free", "last_own", "v", "ou",
    "halves", "q", "v", "k", "near_z", "ou", "k", "ou", "q",
    "near_tied", "v", "k", "q", "v", "k", "ou", "q", "k",
    "v", "ou", "last", "q", "v",
)


def dot(a, b):
    return jnp.dot(a, b, preferred_element_type=F32)


def dot_nt(a, b):
    return lax.dot_general(a, b, (((1,), (1,)), ((), ())), preferred_element_type=F32)


def dot_tn(a, b):
    return lax.dot_general(a, b, (((0,), (0,)), ((), ())), preferred_element_type=F32)


def sigmoid(z):
    return 0.5 + 0.5 * jnp.tanh(0.5 * z)


def norm_rows(z):
    centre = z - jnp.mean(z, axis=-1, keepdims=True)
    inverse = lax.rsqrt(jnp.mean(centre * centre, axis=-1, keepdims=True) + EPS)
    return centre * inverse, inverse


def norm_back(grad, hat, inverse):
    return inverse * (
        grad
        - jnp.mean(grad, axis=-1, keepdims=True)
        - hat * jnp.mean(grad * hat, axis=-1, keepdims=True)
    )


class Net:
    def __init__(self, send_sems, recv_sems):
        self.send_sems, self.recv_sems = send_sems, recv_sems
        self.copies = []

    def send(self, src, dst, device):
        at = len(self.copies)
        copy = pltpu.make_async_remote_copy(
            src_ref=src,
            dst_ref=dst,
            send_sem=self.send_sems.at[at],
            recv_sem=self.recv_sems.at[at],
            device_id=device,
            device_id_type=MESH,
        )
        copy.start()
        self.copies.append((copy, device))
        return at

    def landed(self, at, ref):
        pltpu.make_async_remote_copy(
            src_ref=ref,
            dst_ref=ref,
            send_sem=self.send_sems.at[at],
            recv_sem=self.recv_sems.at[at],
            device_id=self.copies[at][1],
            device_id_type=MESH,
        ).wait_recv()

    def drain(self):
        for copy, _ in self.copies:
            copy.wait_send()


def layer_kernel(
    slots_ref, pattern_ref, length_ref, events, upstream, w_hbm, wo_hbm,
    encoded, grad_events, gw,
    w, wo, gx, normed, own_normed, hat_in, inv_in,
    u_act, u_slope, q_act, q_slope, k_act, k_slope, v_act, v_slope,
    grad_gated, limit_mask, weights, slope, mixed, grad_mixed, grad_q,
    gated, du, dq, dv, dk, own_grad, compact,
    to_sib, from_sib, sum_y, sum_z, r_z2, r_ya, r_yb, r_h, r_p, r_m, r_z0,
    gp, gf, *rest,
):
    ar_bufs, (ar_sems, w_sems, send_sems, recv_sems) = tuple(rest[:-4]), rest[-4:]
    dp = lax.axis_index("dp")
    ctx = lax.axis_index("ctx")
    x, zh = dp // 2, dp % 2
    zl, y, core = ctx // 8, (ctx // 2) % 4, ctx % 2
    z = zh * 2 + zl

    def dev(x, y, z, core):
        return {"dp": x * 2 + z // 2, "ctx": ((z % 2) * 4 + y) * 2 + core}

    def rot(v, by):
        return lax.rem(v + by, 4)

    sib = dev(x, y, z, 1 - core)
    yp, ym, y2 = (dev(x, rot(y, i), z, core) for i in (1, 3, 2))
    zp = dev(x, y, zh * 2 + 1 - zl, core)
    ring_x = [dev(rot(x, i), y, z, core) for i in range(4)]
    ring_y = [dev(x, rot(y, i), z, core) for i in range(4)]
    ring_z = [dev(x, y, rot(z, i), core) for i in range(4)]

    w_copy = pltpu.make_async_copy(w_hbm, w, w_sems.at[0])
    wo_copy = pltpu.make_async_copy(wo_hbm, wo, w_sems.at[1])
    w_copy.start()
    wo_copy.start()

    barrier = pltpu.get_barrier_semaphore()
    partners = [sib] + ring_x[1:] + ring_y[1:] + ring_z[1:]
    for partner in partners:
        pl.semaphore_signal(barrier, inc=1, device_id=partner, device_id_type=MESH)

    net = Net(send_sems, recv_sems)

    def shard(dz, dy, side):
        zz = zl if dz == 0 else 1 - zl
        kk = core if side == 0 else 1 - core
        return ((zz * 4 + rot(y, dy)) * 2 + kk) * 2

    def rows(dz, dy, side=0, half=None):
        base = shard(dz, dy, side)
        if half is None:
            return gx.at[pl.ds(base, 2)]
        return gx.at[base + half]

    for half in range(2):
        gx[shard(0, 0, 0) + half] = events[half * 128 : half * 128 + 128, :]
    pl.semaphore_wait(barrier, len(partners))

    def forward(ref, device):
        return net.send(ref, ref, device)

    a_yp0 = forward(rows(0, 0, 0, 0), yp)
    a_ym0 = forward(rows(0, 0, 0, 1), ym)
    a_z0 = forward(rows(0, 0, 0, 0), zp)
    a_sib = forward(rows(0, 0), sib)
    a_yp1 = forward(rows(0, 0, 0, 1), yp)
    a_ym1 = forward(rows(0, 0, 0, 0), ym)
    a_z1 = forward(rows(0, 0, 0, 1), zp)

    hat, inv = norm_rows(events[...].astype(F32))
    hat_in[...] = hat
    inv_in[...] = inv
    own = hat.astype(BF16)
    own_normed[...] = own
    for b in range(2):
        normed[b * 512 : b * 512 + 128, :] = own[b * 128 : b * 128 + 128]
    w_copy.wait()
    wo_copy.wait()

    def activate(pre):
        sig = sigmoid(pre)
        act = pre * sig
        return act.astype(BF16), sig + act * (1.0 - sig)

    for h in range(4):
        act, sl = activate(dot(own_normed[...], w[:, h * 128 : h * 128 + 128]))
        u_act[h] = act
        u_slope[h] = sl
        act, sl = activate(dot(own_normed[...], w[:, 1024 + h * 128 : 1152 + h * 128]))
        q_act[h] = act
        q_slope[h] = sl

    net.landed(a_yp0, rows(0, 3, 0, 0))
    r_yp = forward(rows(0, 3, 0, 0), yp)
    net.landed(a_ym0, rows(0, 1, 0, 1))
    r_ym = forward(rows(0, 1, 0, 1), ym)
    net.landed(a_z0, rows(1, 0, 0, 0))
    f_yp0 = forward(rows(1, 0, 0, 0), yp)
    f_ym0 = forward(rows(1, 0, 0, 0), ym)

    for h in range(4):
        grad_gated[h] = dot_nt(upstream[...], wo[h * 128 : h * 128 + 128, :])

    def project(lo, n):
        for h in range(4):
            act, sl = activate(dot(normed[pl.ds(lo, n), :], w[:, 512 + h * 128 : 640 + h * 128]))
            v_act[h, pl.ds(lo, n), :] = act
            v_slope[h, pl.ds(lo, n), :] = sl
            act, sl = activate(dot(normed[pl.ds(lo, n), :], w[:, 1536 + h * 128 : 1664 + h * 128]))
            k_act[h, pl.ds(lo, n), :] = act
            k_slope[h, pl.ds(lo, n), :] = sl

    net.landed(a_yp1, rows(0, 3, 0, 1))
    d1 = forward(rows(0, 3), sib)
    net.landed(a_ym1, rows(0, 1, 0, 0))
    d2 = forward(rows(0, 1), sib)
    net.landed(a_z1, rows(1, 0, 0, 1))
    f_yp1 = forward(rows(1, 0, 0, 1), yp)
    f_ym1 = forward(rows(1, 0, 0, 1), ym)
    d3 = forward(rows(1, 0), sib)
    project(0, 128)
    project(512, 128)
    net.landed(r_yp, rows(0, 2, 0, 0))
    z2_0 = forward(rows(0, 2, 0, 0), zp)
    net.landed(r_ym, rows(0, 2, 0, 1))
    z2_1 = forward(rows(0, 2, 0, 1), zp)
    d4 = forward(rows(0, 2), sib)

    length = length_ref[0]
    listed, at_slot, fresh = [], [], []
    for b in range(2):
        mine = slots_ref[2 * ctx + b]
        picks = [mine] + [pattern_ref[t, mine] for t in range(3)]
        listed.append(picks)
        news = [None]
        for t in range(1, 4):
            new = picks[t] != picks[0]
            for s in range(1, t):
                new = jnp.logical_and(new, picks[t] != picks[s])
            news.append(new)
        fresh.append(news)
    found = [[jnp.int32(0)] * 4 for _ in range(2)]
    for s in range(32):
        block = slots_ref[s]
        for b in range(2):
            for t in range(1, 4):
                found[b][t] = jnp.where(block == listed[b][t], s, found[b][t])

    for b in range(2):
        q_pos = listed[b][0] * 128 + lax.broadcasted_iota(jnp.int32, (128, 128), 0)
        top = jnp.where(q_pos < length, q_pos, -1)
        lane = lax.broadcasted_iota(jnp.int32, (128, 128), 1)
        for t in range(4):
            start = listed[b][t] * 128
            if t:
                start = jnp.where(fresh[b][t], start, FAR)
            limit_mask[b, :, t * 128 : t * 128 + 128] = (start + lane <= top).astype(F32)

    net.landed(f_yp0, rows(1, 3, 0, 0))
    net.landed(f_yp1, rows(1, 3, 0, 1))
    d5 = forward(rows(1, 3), sib)
    net.landed(f_ym0, rows(1, 1, 0, 0))
    net.landed(f_ym1, rows(1, 1, 0, 1))
    d6 = forward(rows(1, 1), sib)
    net.landed(z2_0, rows(1, 2, 0, 0))
    net.landed(z2_1, rows(1, 2, 0, 1))
    d7 = forward(rows(1, 2), sib)
    for at, (dz, dy) in zip(
        (a_sib, d1, d2, d3, d4, d5, d6, d7),
        ((0, 0), (0, 3), (0, 1), (1, 0), (0, 2), (1, 3), (1, 1), (1, 2)),
    ):
        net.landed(at, rows(dz, dy, 1))

    for b in range(2):
        for t in range(1, 4):
            block = gx[found[b][t]]
            normed[b * 512 + t * 128 : b * 512 + t * 128 + 128, :] = norm_rows(block.astype(F32))[
                0
            ].astype(BF16)
    project(128, 384)
    project(640, 384)

    def forward_head(i, carry):
        b, h = i // 4, i % 4
        q = q_act[h, pl.ds(pl.multiple_of(b * 128, 128), 128), :]
        for t in range(4):
            lo = pl.multiple_of(b * 512 + t * 128, 128)
            s = dot_nt(q, k_act[h, pl.ds(lo, 128), :]) * SCALE
            mask = limit_mask[b, :, t * 128 : t * 128 + 128]
            sig = sigmoid(s)
            act = s * sig
            weights[i, :, t * 128 : t * 128 + 128] = (act * mask).astype(BF16)
            slope[i, :, t * 128 : t * 128 + 128] = (sig + act * (1.0 - sig)) * (mask * SCALE)
        mixed[h, pl.ds(pl.multiple_of(b * 128, 128), 128), :] = dot(
            weights[i], v_act[h, pl.ds(pl.multiple_of(b * 512, 512), 512), :]
        )
        return carry

    lax.fori_loop(0, 8, forward_head, 0, unroll=8)

    def across(parts):
        return sum(jnp.sum(part, axis=-1, keepdims=True) for part in parts) * (1.0 / D)

    parts = [mixed[h] for h in range(4)]
    mean = across(parts)
    parts = [part - mean for part in parts]
    inv_mix = lax.rsqrt(across([part * part for part in parts]) + EPS)
    hats = [part * inv_mix for part in parts]
    us = [u_act[h].astype(F32) for h in range(4)]
    gated[...] = jnp.concatenate([(hats[h] * us[h]).astype(BF16) for h in range(4)], axis=1)
    ggs = [grad_gated[h] for h in range(4)]
    du[...] = jnp.concatenate(
        [(ggs[h] * hats[h] * u_slope[h]).astype(BF16) for h in range(4)], axis=1
    )
    ts = [ggs[h] * us[h] for h in range(4)]
    mean_t = across(ts)
    mean_th = across([ts[h] * hats[h] for h in range(4)])
    for h in range(4):
        grad_mixed[h] = (inv_mix * (ts[h] - mean_t - hats[h] * mean_th)).astype(BF16)
    gp[:, G_OUT : G_OUT + 512] = dot_tn(gated[...], upstream[...]).astype(BF16)
    gp[:, G_U : G_U + 512] = dot_tn(own_normed[...], du[...]).astype(BF16)

    place = {"x": x, "y": y, "z": z}
    rings = {"x": ring_x, "y": ring_y, "z": ring_z}

    def span(start, n):
        return pl.ds(pl.multiple_of(start, n), n)

    def add4(parts):
        return sum(part.astype(F32) for part in parts).astype(BF16)

    def reduce_columns(lo, n, axes, bufs):
        sibling, first, second, third, total, local_sem = bufs
        a1, a2, a3 = axes
        p1, p2, p3 = (place[a] for a in axes)
        half = n // 2
        mine = pl.ds(pl.multiple_of(lo + core * half, 128), half)
        other = pl.ds(pl.multiple_of(lo + (1 - core) * half, 128), half)
        far_first, near_first = (1, 3, 2), (3, 1, 2)

        def rows1(p):
            return span(p * 128, 128)

        def rows2(p):
            return span(p1 * 128 + p * 32, 32)

        at = net.send(gp.at[:, other], sibling, sib)
        yield
        net.landed(at, sibling)
        ats = []
        for i in far_first + (0,):
            block = rows1(rot(p1, i))
            sibling[block, :] = gp[block, mine] + sibling[block, :]
            if i:
                ats.append(net.send(sibling.at[block], first.at[i], rings[a1][i]))
        yield
        for at, i in zip(ats, far_first):
            net.landed(at, first.at[i])
        first[0] = add4([sibling[rows1(p1), :], first[1], first[2], first[3]])
        ats = [
            net.send(first.at[0, span(rot(p2, i) * 32, 32)], second.at[i], rings[a2][i])
            for i in far_first
        ]
        yield
        for at, i in zip(ats, far_first):
            net.landed(at, second.at[i])
        total[...] = add4([first[0, span(p2 * 32, 32), :], second[1], second[2], second[3]])
        third[p3] = total[...]
        ats = [net.send(total, third.at[p3], rings[a3][i]) for i in far_first]
        yield
        for at, i in zip(ats, near_first):
            net.landed(at, third.at[rot(p3, i)])
        gf[rows2(p2), mine] = add4([third[0], third[1], third[2], third[3]])
        here = gf.at[rows2(p2), mine]
        ats = [net.send(here, here, rings[a2][i]) for i in far_first]
        yield
        for at, i in zip(ats, near_first):
            net.landed(at, gf.at[rows2(rot(p2, i)), mine])
        here, there = gf.at[rows1(p1), mine], gw.at[rows1(p1), mine]
        ats = [net.send(here, there, rings[a1][i]) for i in far_first]
        back = [net.send(here, there, sib)]
        keep = pltpu.make_async_copy(here, there, local_sem)
        keep.start()
        yield
        for at, i in zip(ats, near_first):
            there = gw.at[rows1(rot(p1, i)), mine]
            net.landed(at, there)
            back.append(net.send(there, there, sib))
        yield
        for at, i in zip(back, (0,) + near_first):
            net.landed(at, gw.at[rows1(rot(p1, i)), other])
        keep.wait()
        yield

    parts = {
        name: reduce_columns(lo, n, axes, ar_bufs[5 * i : 5 * i + 5] + (ar_sems.at[i],))
        for i, (name, lo, n, axes) in enumerate(PARTS)
    }

    def heads_of(ref):
        return jnp.concatenate([ref[h] for h in range(4)], axis=1)

    def value_head(i, carry):
        b, h = i // 4, i % 4
        k_rows = pl.ds(pl.multiple_of(b * 512, 512), 512)
        gm = grad_mixed[h, pl.ds(pl.multiple_of(b * 128, 128), 128), :]
        dv[h, k_rows, :] = (dot_tn(weights[i], gm) * v_slope[h, k_rows, :]).astype(BF16)
        return carry

    def value_heads():
        lax.fori_loop(0, 8, value_head, 0, unroll=8)

    def weight_v():
        gp[:, G_V : G_V + 512] = dot_tn(normed[...], heads_of(dv)).astype(BF16)

    def score_head(i, carry):
        b, h = i // 4, i % 4
        q_rows = pl.ds(pl.multiple_of(b * 128, 128), 128)
        k_rows = pl.ds(pl.multiple_of(b * 512, 512), 512)
        gm = grad_mixed[h, q_rows, :]
        q = q_act[h, q_rows, :]
        gs = (dot_nt(gm, v_act[h, k_rows, :]) * slope[i]).astype(BF16)
        grad_q[h, q_rows, :] = dot(gs, k_act[h, k_rows, :])
        dk[h, k_rows, :] = (dot_tn(gs, q) * k_slope[h, k_rows, :]).astype(BF16)
        return carry

    def score_heads():
        lax.fori_loop(0, 8, score_head, 0, unroll=8)

    def weight_k():
        gp[:, G_K : G_K + 512] = dot_tn(normed[...], heads_of(dk)).astype(BF16)

    def weight_q():
        dq[...] = jnp.concatenate(
            [(grad_q[h] * q_slope[h]).astype(BF16) for h in range(4)], axis=1
        )
        gp[:, G_Q : G_Q + 512] = dot_tn(own_normed[...], dq[...]).astype(BF16)

    def back_rows():
        back = dot_nt(heads_of(dv), w[:, 512:1024]) + dot_nt(heads_of(dk), w[:, 1536:2048])
        for b in range(2):
            for t in range(1, 4):
                lo = b * 512 + t * 128
                compact[b * 3 + t - 1] = back[lo : lo + 128].astype(BF16)
            own_grad[b * 128 : b * 128 + 128, :] = back[b * 512 : b * 512 + 128]
        compact[6] = jnp.zeros((128, 512), BF16)

    def encode():
        encoded[...] = (events[...].astype(F32) + dot(gated[...], wo[...])).astype(BF16)

    def own_rows():
        own_grad[...] += dot_nt(du[...], w[:, 0:512]) + dot_nt(dq[...], w[:, 1024:1536])

    def piece(dz, dy, side, half):
        zz = zl if dz == 0 else 1 - zl
        kk = core if side == 0 else 1 - core
        slot = ((zz * 4 + rot(y, dy)) * 2 + kk) * 2 + half
        both = []
        for b in range(2):
            at = jnp.int32(6)
            for t in range(1, 4):
                hit = jnp.logical_and(found[b][t] == slot, fresh[b][t])
                at = jnp.where(hit, b * 3 + t - 1, at)
            both.append(compact[at])
        return both[0] + both[1]

    HALF = (pl.ds(0, 128), pl.ds(128, 128))
    sib_at, sib_here, sent = {}, set(), {}

    def to_sibling(order):
        for dz, dy in order:
            j = dz * 4 + dy
            for half in range(2):
                to_sib[j, HALF[half], :] = piece(dz, dy, 1, half)
            sib_at[j] = net.send(to_sib.at[j], from_sib.at[j], sib)

    def chip_sum(dz, dy, half):
        j = dz * 4 + dy
        if j not in sib_here:
            net.landed(sib_at[j], from_sib.at[j])
            sib_here.add(j)
        return piece(dz, dy, 0, half) + from_sib[j, HALF[half], :]

    def pass_on(name, buf, dz, dy, half, there, device, extra=()):
        total = chip_sum(dz, dy, half)
        for other_name, ref in extra:
            net.landed(sent[other_name, half], ref)
            total = total + ref[...]
        buf[HALF[half], :] = total
        sent[name, half] = net.send(buf.at[HALF[half]], there, device)

    def d2d_a():
        to_sibling(((1, 2), (1, 1), (1, 3)))

    def d2d_b():
        to_sibling(((0, 2), (1, 0), (0, 1), (0, 3), (0, 0)))

    def far_z():
        for half in range(2):
            pass_on("z2", sum_z.at[0], 1, 2, half, r_z2.at[HALF[half]], zp)

    def far_y():
        for half in range(2):
            pass_on("ya", sum_y.at[0], 1, 1, half, r_ya.at[HALF[half]], yp)
            pass_on("yb", sum_y.at[1], 1, 3, half, r_yb.at[HALF[half]], ym)

    def near_free():
        pass_on("p", sum_y.at[3], 0, 1, 1, r_p.at[HALF[1]], yp)
        pass_on("m", sum_y.at[4], 0, 3, 0, r_m.at[HALF[0]], ym)

    def halves():
        for half in range(2):
            pass_on(
                "h", sum_y.at[2], 0, 2, half, r_h.at[half], (yp, ym)[half],
                (("z2", r_z2.at[HALF[half]]),),
            )

    def near_z():
        for half in range(2):
            pass_on(
                "z0", sum_z.at[1], 1, 0, half, r_z0.at[HALF[half]], zp,
                (("ya", r_ya.at[HALF[half]]), ("yb", r_yb.at[HALF[half]])),
            )

    def near_tied():
        pass_on("p", sum_y.at[3], 0, 1, 0, r_p.at[HALF[0]], yp, (("h", r_h.at[0]),))
        pass_on("m", sum_y.at[4], 0, 3, 1, r_m.at[HALF[1]], ym, (("h", r_h.at[1]),))

    def last_own():
        for half in range(2):
            own_grad[HALF[half], :] += chip_sum(0, 0, half).astype(F32)

    def last():
        for half in range(2):
            total = own_grad[HALF[half], :]
            for name, ref in (("p", r_p), ("m", r_m), ("z0", r_z0)):
                net.landed(sent[name, half], ref.at[HALF[half]])
                total = total + ref[HALF[half], :].astype(F32)
            grad_events[HALF[half], :] = (
                upstream[HALF[half], :].astype(F32)
                + norm_back(total, hat_in[HALF[half], :], inv_in[HALF[half], :])
            ).astype(BF16)

    steps = dict(
        value_heads=value_heads, weight_v=weight_v, score_heads=score_heads, weight_k=weight_k,
        weight_q=weight_q, back_rows=back_rows, encode=encode, own_rows=own_rows, d2d_a=d2d_a,
        d2d_b=d2d_b, far_z=far_z, far_y=far_y, near_free=near_free, halves=halves,
        near_z=near_z, near_tied=near_tied, last_own=last_own, last=last,
    )
    for step in SCHEDULE:
        if step in parts:
            next(parts[step])
        else:
            steps[step]()
    net.drain()


def finish_kernel(
    gw, enc, gev, grad_in, grad_out, encoded, grad_events, got, full, rest, in_sems, out_sems
):
    rows = [pl.ds(i * 128, 128) for i in range(4)]
    reads = [pltpu.make_async_copy(gw.at[r], got.at[r], in_sems.at[i]) for i, r in enumerate(rows)]
    reads += [
        pltpu.make_async_copy(enc, rest.at[0], in_sems.at[4]),
        pltpu.make_async_copy(gev, rest.at[1], in_sems.at[5]),
    ]
    for copy in reads:
        copy.start()
    writes = []
    for i, r in enumerate(rows):
        reads[i].wait()
        full[r, :] = got[r, :].astype(F32)
        writes += [
            pltpu.make_async_copy(full.at[r, pl.ds(512, 2048)], grad_in.at[r], out_sems.at[i]),
            pltpu.make_async_copy(full.at[r, pl.ds(0, 512)], grad_out.at[r], out_sems.at[4 + i]),
        ]
        for copy in writes[-2:]:
            copy.start()
    for i, (copy, out) in enumerate(zip(reads[4:], (encoded, grad_events))):
        copy.wait()
        writes.append(pltpu.make_async_copy(rest.at[i], out, out_sems.at[8 + i]))
        writes[-1].start()
    for copy in writes:
        copy.wait()


def finish(gw, enc, gev):
    hbm = pl.BlockSpec(memory_space=pl.ANY)
    return pl.pallas_call(
        finish_kernel,
        out_shape=(
            jax.ShapeDtypeStruct((512, 2048), F32),
            jax.ShapeDtypeStruct((512, 512), F32),
            jax.ShapeDtypeStruct((256, D), BF16),
            jax.ShapeDtypeStruct((256, D), BF16),
        ),
        in_specs=[hbm] * 3,
        out_specs=(hbm,) * 4,
        scratch_shapes=[
            pltpu.VMEM((512, GCOLS), BF16),
            pltpu.VMEM((512, GCOLS), F32),
            pltpu.VMEM((2, 256, D), BF16),
            pltpu.SemaphoreType.DMA((6,)),
            pltpu.SemaphoreType.DMA((10,)),
        ],
        compiler_params=pltpu.CompilerParams(vmem_limit_bytes=60 * 2**20),
        name="finish",
    )(gw, enc, gev)


def local(events, upstream, lengths, block_slots, pattern, in_weight, out_weight):
    vmem = pl.BlockSpec(memory_space=pltpu.VMEM)
    smem = pl.BlockSpec(memory_space=pltpu.SMEM)
    hbm = pl.BlockSpec(memory_space=pl.ANY)
    v = pltpu.VMEM
    scratch = [
        v((512, 2048), BF16), v((512, 512), BF16), v((32, 128, 512), BF16),
        v((1024, 512), BF16), v((256, 512), BF16), v((256, 512), F32), v((256, 1), F32),
        v((4, 256, 128), BF16), v((4, 256, 128), F32),
        v((4, 256, 128), BF16), v((4, 256, 128), F32),
        v((4, 1024, 128), BF16), v((4, 1024, 128), F32),
        v((4, 1024, 128), BF16), v((4, 1024, 128), F32),
        v((4, 256, 128), F32), v((2, 128, 512), F32), v((8, 128, 512), BF16),
        v((8, 128, 512), F32), v((4, 256, 128), F32), v((4, 256, 128), BF16),
        v((4, 256, 128), F32),
        v((256, 512), BF16), v((256, 512), BF16), v((256, 512), BF16),
        v((4, 1024, 128), BF16), v((4, 1024, 128), BF16), v((256, 512), F32),
        v((7, 128, 512), BF16),
        v((8, 256, 512), BF16), v((8, 256, 512), BF16), v((5, 256, 512), BF16),
        v((2, 256, 512), BF16),
        v((256, 512), BF16), v((256, 512), BF16), v((256, 512), BF16), v((2, 128, 512), BF16),
        v((256, 512), BF16), v((256, 512), BF16), v((256, 512), BF16),
        v((512, GCOLS), BF16), v((512, GCOLS), BF16),
    ]
    for _, _, columns, _ in PARTS:
        half = columns // 2
        scratch += [
            v((512, half), BF16), v((4, 128, half), BF16), v((4, 32, half), BF16),
            v((4, 32, half), BF16), v((32, half), BF16),
        ]
    scratch += [
        pltpu.SemaphoreType.DMA((len(PARTS),)),
        pltpu.SemaphoreType.DMA((2,)),
        pltpu.SemaphoreType.DMA((N_SEM,)),
        pltpu.SemaphoreType.DMA((N_SEM,)),
    ]
    encoded, grad_events, gw = pl.pallas_call(
        layer_kernel,
        out_shape=(
            jax.ShapeDtypeStruct((256, D), BF16),
            jax.ShapeDtypeStruct((256, D), BF16),
            jax.ShapeDtypeStruct((512, GCOLS), BF16),
        ),
        in_specs=[smem, smem, smem, vmem, vmem, hbm, hbm],
        out_specs=(vmem, vmem, hbm),
        scratch_shapes=scratch,
        compiler_params=pltpu.CompilerParams(
            collective_id=0, has_side_effects=True, vmem_limit_bytes=56 * 2**20
        ),
        name="layer",
    )(block_slots, pattern.T, lengths, events[0], upstream[0], in_weight, out_weight)
    grad_in, grad_out, encoded, grad_events = finish(gw, encoded, grad_events)
    return encoded[None], grad_events[None], grad_in, grad_out


def solution(mesh):
    return jax.shard_map(
        local,
        mesh=mesh,
        in_specs=(P("dp", "ctx", None), P("dp", "ctx", None), P("dp"), P(), P(), P(), P()),
        out_specs=(P("dp", "ctx", None), P("dp", "ctx", None), P(), P()),
        check_vma=False,
    )
```

```python
import functools

import jax
import jax.numpy as jnp
from jax import lax
from jax.experimental import pallas as pl
from jax.experimental.pallas import tpu as pltpu
from jax.sharding import PartitionSpec as P

HEADS = 4
HD = 128
BLK = 128
D = 512
EPS = 1e-05
SCALE = HD ** (-0.5)
MESH = pl.DeviceIdType.MESH
F32 = jnp.float32
BF16 = jnp.bfloat16
FAR = 1 << 20
G_OUT, G_U, G_V, G_Q, G_K = 0, 512, 1024, 1536, 2048
GCOLS = 2560
N_SEM = 176
PARTS = (
    ("ou", G_OUT, 1024, ("y", "x", "z")),
    ("v", G_V, 512, ("x", "z", "y")),
    ("k", G_K, 512, ("x", "y", "z")),
    ("q", G_Q, 512, ("z", "x", "y")),
)
SCHEDULE = (
    "ou", "value_heads", "score_heads", "ou", "weight_k", "weight_q", "weight_v", "v",
    "q", "k", "back_rows", "d2d_a", "q", "k", "v", "far_z0",
    "far_z1", "far_y0", "far_y1", "d2d_b", "ou", "q", "k", "own_rows",
    "encode", "near_free", "last_own", "v", "ou", "middle0", "middle1", "q",
    "v", "k", "near_z0", "near_z1", "ou", "k", "ou", "q",
    "near_p", "near_m", "v", "k", "q", "v", "k", "ou",
    "q", "k", "v", "ou", "last", "q", "v",
)


def dot(a, b):
    return jnp.dot(a, b, preferred_element_type=F32)


def dot_nt(a, b):
    return lax.dot_general(a, b, (((1,), (1,)), ((), ())), preferred_element_type=F32)


def dot_tn(a, b):
    return lax.dot_general(a, b, (((0,), (0,)), ((), ())), preferred_element_type=F32)


def sigmoid(z):
    return 0.5 + 0.5 * jnp.tanh(0.5 * z)


def norm_rows(z):
    centre = z - jnp.mean(z, axis=-1, keepdims=True)
    inverse = lax.rsqrt(jnp.mean(centre * centre, axis=-1, keepdims=True) + EPS)
    return centre * inverse, inverse


def norm_back(grad, hat, inverse):
    return inverse * (
        grad
        - jnp.mean(grad, axis=-1, keepdims=True)
        - hat * jnp.mean(grad * hat, axis=-1, keepdims=True)
    )


class Net:
    def __init__(self, send_sems, recv_sems):
        self.send_sems, self.recv_sems = send_sems, recv_sems
        self.copies = []

    def send(self, src, dst, device):
        at = len(self.copies)
        copy = pltpu.make_async_remote_copy(
            src_ref=src,
            dst_ref=dst,
            send_sem=self.send_sems.at[at],
            recv_sem=self.recv_sems.at[at],
            device_id=device,
            device_id_type=MESH,
        )
        copy.start()
        self.copies.append((copy, device))
        return at

    def landed(self, at, ref):
        pltpu.make_async_remote_copy(
            src_ref=ref,
            dst_ref=ref,
            send_sem=self.send_sems.at[at],
            recv_sem=self.recv_sems.at[at],
            device_id=self.copies[at][1],
            device_id_type=MESH,
        ).wait_recv()

    def drain(self):
        for copy, _ in self.copies:
            copy.wait_send()


def layer_kernel(
    slots_ref, pattern_ref, length_ref, events, upstream, w_hbm, wo_hbm,
    encoded, grad_events, gw,
    w, wo, gx, normed, own_normed, hat_in, inv_in,
    u_act, u_slope, q_act, q_slope, k_act, k_slope, v_act, v_slope,
    grad_gated, limit_mask, weights, slope, mixed, grad_mixed, grad_q,
    gated, du, dq, dv, dk, own_grad, compact,
    to_sib, from_sib, sum_y, sum_z, r_z2, r_ya, r_yb, r_h, r_p, r_m, r_z0,
    gp, *rest,
):
    ar_bufs, (w_sems, send_sems, recv_sems) = rest[:-3], rest[-3:]
    dp = lax.axis_index("dp")
    ctx = lax.axis_index("ctx")
    x, zh = dp // 2, dp % 2
    zl, y, core = ctx // 8, (ctx // 2) % 4, ctx % 2
    z = zh * 2 + zl

    def dev(x, y, z, core):
        return {"dp": x * 2 + z // 2, "ctx": ((z % 2) * 4 + y) * 2 + core}

    def rot(v, by):
        return lax.rem(v + by, 4)

    sib = dev(x, y, z, 1 - core)
    yp, ym, y2 = (dev(x, rot(y, i), z, core) for i in (1, 3, 2))
    zp = dev(x, y, zh * 2 + 1 - zl, core)
    ring_x = [dev(rot(x, i), y, z, core) for i in range(4)]
    ring_y = [dev(x, rot(y, i), z, core) for i in range(4)]
    ring_z = [dev(x, y, rot(z, i), core) for i in range(4)]

    w_copy = pltpu.make_async_copy(w_hbm, w, w_sems.at[0])
    wo_copy = pltpu.make_async_copy(wo_hbm, wo, w_sems.at[1])
    w_copy.start()
    wo_copy.start()

    barrier = pltpu.get_barrier_semaphore()
    partners = [sib] + ring_x[1:] + ring_y[1:] + ring_z[1:]
    for partner in partners:
        pl.semaphore_signal(barrier, inc=1, device_id=partner, device_id_type=MESH)

    net = Net(send_sems, recv_sems)

    def shard(dz, dy, side):
        zz = zl if dz == 0 else 1 - zl
        kk = core if side == 0 else 1 - core
        return ((zz * 4 + rot(y, dy)) * 2 + kk) * 2

    def rows(dz, dy, side=0, half=None):
        base = shard(dz, dy, side)
        if half is None:
            return gx.at[pl.ds(base, 2)]
        return gx.at[base + half]

    for half in range(2):
        gx[shard(0, 0, 0) + half] = events[half * 128 : half * 128 + 128, :]
    pl.semaphore_wait(barrier, len(partners))

    def forward(ref, device):
        return net.send(ref, ref, device)

    a_yp0 = forward(rows(0, 0, 0, 0), yp)
    a_ym0 = forward(rows(0, 0, 0, 1), ym)
    a_z0 = forward(rows(0, 0, 0, 0), zp)
    a_sib = forward(rows(0, 0), sib)
    a_yp1 = forward(rows(0, 0, 0, 1), yp)
    a_ym1 = forward(rows(0, 0, 0, 0), ym)
    a_z1 = forward(rows(0, 0, 0, 1), zp)

    hat, inv = norm_rows(events[...].astype(F32))
    hat_in[...] = hat
    inv_in[...] = inv
    own = hat.astype(BF16)
    own_normed[...] = own
    for b in range(2):
        normed[b * 512 : b * 512 + 128, :] = own[b * 128 : b * 128 + 128]
    w_copy.wait()
    wo_copy.wait()

    def activate(pre):
        sig = sigmoid(pre)
        act = pre * sig
        return act.astype(BF16), sig + act * (1.0 - sig)

    for h in range(4):
        act, sl = activate(dot(own_normed[...], w[:, h * 128 : h * 128 + 128]))
        u_act[h] = act
        u_slope[h] = sl
        act, sl = activate(dot(own_normed[...], w[:, 1024 + h * 128 : 1152 + h * 128]))
        q_act[h] = act
        q_slope[h] = sl

    net.landed(a_yp0, rows(0, 3, 0, 0))
    r_yp = forward(rows(0, 3, 0, 0), yp)
    net.landed(a_ym0, rows(0, 1, 0, 1))
    r_ym = forward(rows(0, 1, 0, 1), ym)
    net.landed(a_z0, rows(1, 0, 0, 0))
    f_yp0 = forward(rows(1, 0, 0, 0), yp)
    f_ym0 = forward(rows(1, 0, 0, 0), ym)

    for h in range(4):
        grad_gated[h] = dot_nt(upstream[...], wo[h * 128 : h * 128 + 128, :])

    def project(lo, n):
        for h in range(4):
            act, sl = activate(dot(normed[pl.ds(lo, n), :], w[:, 512 + h * 128 : 640 + h * 128]))
            v_act[h, pl.ds(lo, n), :] = act
            v_slope[h, pl.ds(lo, n), :] = sl
            act, sl = activate(dot(normed[pl.ds(lo, n), :], w[:, 1536 + h * 128 : 1664 + h * 128]))
            k_act[h, pl.ds(lo, n), :] = act
            k_slope[h, pl.ds(lo, n), :] = sl

    net.landed(a_yp1, rows(0, 3, 0, 1))
    d1 = forward(rows(0, 3), sib)
    net.landed(a_ym1, rows(0, 1, 0, 0))
    d2 = forward(rows(0, 1), sib)
    net.landed(a_z1, rows(1, 0, 0, 1))
    f_yp1 = forward(rows(1, 0, 0, 1), yp)
    f_ym1 = forward(rows(1, 0, 0, 1), ym)
    d3 = forward(rows(1, 0), sib)
    project(0, 128)
    project(512, 128)
    net.landed(r_yp, rows(0, 2, 0, 0))
    z2_0 = forward(rows(0, 2, 0, 0), zp)
    net.landed(r_ym, rows(0, 2, 0, 1))
    z2_1 = forward(rows(0, 2, 0, 1), zp)
    d4 = forward(rows(0, 2), sib)

    length = length_ref[0]
    listed, at_slot, fresh = [], [], []
    for b in range(2):
        mine = slots_ref[2 * ctx + b]
        picks = [mine] + [pattern_ref[t, mine] for t in range(3)]
        listed.append(picks)
        news = [None]
        for t in range(1, 4):
            new = picks[t] != picks[0]
            for s in range(1, t):
                new = jnp.logical_and(new, picks[t] != picks[s])
            news.append(new)
        fresh.append(news)
    found = [[jnp.int32(0)] * 4 for _ in range(2)]
    for s in range(32):
        block = slots_ref[s]
        for b in range(2):
            for t in range(1, 4):
                found[b][t] = jnp.where(block == listed[b][t], s, found[b][t])

    for b in range(2):
        q_pos = listed[b][0] * 128 + lax.broadcasted_iota(jnp.int32, (128, 128), 0)
        top = jnp.where(q_pos < length, q_pos, -1)
        lane = lax.broadcasted_iota(jnp.int32, (128, 128), 1)
        for t in range(4):
            start = listed[b][t] * 128
            if t:
                start = jnp.where(fresh[b][t], start, FAR)
            limit_mask[b, :, t * 128 : t * 128 + 128] = (start + lane <= top).astype(F32)

    net.landed(f_yp0, rows(1, 3, 0, 0))
    net.landed(f_yp1, rows(1, 3, 0, 1))
    d5 = forward(rows(1, 3), sib)
    net.landed(f_ym0, rows(1, 1, 0, 0))
    net.landed(f_ym1, rows(1, 1, 0, 1))
    d6 = forward(rows(1, 1), sib)
    net.landed(z2_0, rows(1, 2, 0, 0))
    net.landed(z2_1, rows(1, 2, 0, 1))
    d7 = forward(rows(1, 2), sib)
    for at, (dz, dy) in zip(
        (a_sib, d1, d2, d3, d4, d5, d6, d7),
        ((0, 0), (0, 3), (0, 1), (1, 0), (0, 2), (1, 3), (1, 1), (1, 2)),
    ):
        net.landed(at, rows(dz, dy, 1))

    for b in range(2):
        for t in range(1, 4):
            block = gx[found[b][t]]
            normed[b * 512 + t * 128 : b * 512 + t * 128 + 128, :] = norm_rows(block.astype(F32))[
                0
            ].astype(BF16)
    project(128, 384)
    project(640, 384)

    def forward_head(i, carry):
        b, h = i // 4, i % 4
        q = q_act[h, pl.ds(pl.multiple_of(b * 128, 128), 128), :]
        for t in range(4):
            lo = pl.multiple_of(b * 512 + t * 128, 128)
            s = dot_nt(q, k_act[h, pl.ds(lo, 128), :]) * SCALE
            mask = limit_mask[b, :, t * 128 : t * 128 + 128]
            sig = sigmoid(s)
            act = s * sig
            weights[i, :, t * 128 : t * 128 + 128] = (act * mask).astype(BF16)
            slope[i, :, t * 128 : t * 128 + 128] = (sig + act * (1.0 - sig)) * (mask * SCALE)
        mixed[h, pl.ds(pl.multiple_of(b * 128, 128), 128), :] = dot(
            weights[i], v_act[h, pl.ds(pl.multiple_of(b * 512, 512), 512), :]
        )
        return carry

    lax.fori_loop(0, 8, forward_head, 0, unroll=8)

    def across(parts):
        return sum(jnp.sum(part, axis=-1, keepdims=True) for part in parts) * (1.0 / D)

    parts = [mixed[h] for h in range(4)]
    mean = across(parts)
    parts = [part - mean for part in parts]
    inv_mix = lax.rsqrt(across([part * part for part in parts]) + EPS)
    hats = [part * inv_mix for part in parts]
    us = [u_act[h].astype(F32) for h in range(4)]
    gated[...] = jnp.concatenate([(hats[h] * us[h]).astype(BF16) for h in range(4)], axis=1)
    ggs = [grad_gated[h] for h in range(4)]
    du[...] = jnp.concatenate(
        [(ggs[h] * hats[h] * u_slope[h]).astype(BF16) for h in range(4)], axis=1
    )
    ts = [ggs[h] * us[h] for h in range(4)]
    mean_t = across(ts)
    mean_th = across([ts[h] * hats[h] for h in range(4)])
    for h in range(4):
        grad_mixed[h] = (inv_mix * (ts[h] - mean_t - hats[h] * mean_th)).astype(BF16)
    gp[:, G_OUT : G_OUT + 512] = dot_tn(gated[...], upstream[...]).astype(BF16)
    gp[:, G_U : G_U + 512] = dot_tn(own_normed[...], du[...]).astype(BF16)

    place = {"x": x, "y": y, "z": z}
    rings = {"x": ring_x, "y": ring_y, "z": ring_z}

    def span(start, n):
        return pl.ds(pl.multiple_of(start, n), n)

    def add4(parts):
        return sum(part.astype(F32) for part in parts).astype(BF16)

    def reduce_columns(lo, n, axes, bufs):
        sibling, first, second, third, total = bufs
        a1, a2, a3 = axes
        p1, p2, p3 = (place[a] for a in axes)
        half = n // 2
        mine = pl.ds(pl.multiple_of(lo + core * half, 128), half)
        other = pl.ds(pl.multiple_of(lo + (1 - core) * half, 128), half)
        far_first, near_first = (1, 3, 2), (3, 1, 2)

        def rows1(p):
            return span(p * 128, 128)

        def rows2(p):
            return span(p1 * 128 + p * 32, 32)

        at = net.send(gp.at[:, other], sibling, sib)
        yield
        net.landed(at, sibling)
        ats = []
        for i in far_first + (0,):
            block = rows1(rot(p1, i))
            sibling[block, :] = gp[block, mine] + sibling[block, :]
            if i:
                ats.append(net.send(sibling.at[block], first.at[i], rings[a1][i]))
        yield
        for at, i in zip(ats, far_first):
            net.landed(at, first.at[i])
        first[0] = add4([sibling[rows1(p1), :], first[1], first[2], first[3]])
        ats = [
            net.send(first.at[0, span(rot(p2, i) * 32, 32)], second.at[i], rings[a2][i])
            for i in far_first
        ]
        yield
        for at, i in zip(ats, far_first):
            net.landed(at, second.at[i])
        total[...] = add4([first[0, span(p2 * 32, 32), :], second[1], second[2], second[3]])
        third[p3] = total[...]
        ats = [net.send(total, third.at[p3], rings[a3][i]) for i in far_first]
        yield
        for at, i in zip(ats, near_first):
            net.landed(at, third.at[rot(p3, i)])
        gw[rows2(p2), mine] = add4([third[0], third[1], third[2], third[3]])
        here = gw.at[rows2(p2), mine]
        ats = [net.send(here, here, rings[a2][i]) for i in far_first]
        yield
        for at, i in zip(ats, near_first):
            net.landed(at, gw.at[rows2(rot(p2, i)), mine])
        here = gw.at[rows1(p1), mine]
        ats = [net.send(here, here, rings[a1][i]) for i in far_first]
        back = [net.send(here, here, sib)]
        yield
        for at, i in zip(ats, near_first):
            there = gw.at[rows1(rot(p1, i)), mine]
            net.landed(at, there)
            back.append(net.send(there, there, sib))
        yield
        for at, i in zip(back, (0,) + near_first):
            net.landed(at, gw.at[rows1(rot(p1, i)), other])
        yield

    parts = {
        name: reduce_columns(lo, n, axes, ar_bufs[5 * i : 5 * i + 5])
        for i, (name, lo, n, axes) in enumerate(PARTS)
    }

    def heads_of(ref):
        return jnp.concatenate([ref[h] for h in range(4)], axis=1)

    def value_head(i, carry):
        b, h = i // 4, i % 4
        k_rows = pl.ds(pl.multiple_of(b * 512, 512), 512)
        gm = grad_mixed[h, pl.ds(pl.multiple_of(b * 128, 128), 128), :]
        dv[h, k_rows, :] = (dot_tn(weights[i], gm) * v_slope[h, k_rows, :]).astype(BF16)
        return carry

    def value_heads():
        lax.fori_loop(0, 8, value_head, 0, unroll=8)

    def weight_v():
        gp[:, G_V : G_V + 512] = dot_tn(normed[...], heads_of(dv)).astype(BF16)

    def score_head(i, carry):
        b, h = i // 4, i % 4
        q_rows = pl.ds(pl.multiple_of(b * 128, 128), 128)
        k_rows = pl.ds(pl.multiple_of(b * 512, 512), 512)
        gm = grad_mixed[h, q_rows, :]
        q = q_act[h, q_rows, :]
        gs = (dot_nt(gm, v_act[h, k_rows, :]) * slope[i]).astype(BF16)
        grad_q[h, q_rows, :] = dot(gs, k_act[h, k_rows, :])
        dk[h, k_rows, :] = (dot_tn(gs, q) * k_slope[h, k_rows, :]).astype(BF16)
        return carry

    def score_heads():
        lax.fori_loop(0, 8, score_head, 0, unroll=8)

    def weight_k():
        gp[:, G_K : G_K + 512] = dot_tn(normed[...], heads_of(dk)).astype(BF16)

    def weight_q():
        dq[...] = jnp.concatenate(
            [(grad_q[h] * q_slope[h]).astype(BF16) for h in range(4)], axis=1
        )
        gp[:, G_Q : G_Q + 512] = dot_tn(own_normed[...], dq[...]).astype(BF16)

    def back_rows():
        back = dot_nt(heads_of(dv), w[:, 512:1024]) + dot_nt(heads_of(dk), w[:, 1536:2048])
        for b in range(2):
            for t in range(1, 4):
                lo = b * 512 + t * 128
                compact[b * 3 + t - 1] = back[lo : lo + 128].astype(BF16)
            own_grad[b * 128 : b * 128 + 128, :] = back[b * 512 : b * 512 + 128]
        compact[6] = jnp.zeros((128, 512), BF16)

    def encode():
        encoded[...] = (events[...].astype(F32) + dot(gated[...], wo[...])).astype(BF16)

    def own_rows():
        own_grad[...] += dot_nt(du[...], w[:, 0:512]) + dot_nt(dq[...], w[:, 1024:1536])

    def piece(dz, dy, side, half):
        zz = zl if dz == 0 else 1 - zl
        kk = core if side == 0 else 1 - core
        slot = ((zz * 4 + rot(y, dy)) * 2 + kk) * 2 + half
        both = []
        for b in range(2):
            at = jnp.int32(6)
            for t in range(1, 4):
                hit = jnp.logical_and(found[b][t] == slot, fresh[b][t])
                at = jnp.where(hit, b * 3 + t - 1, at)
            both.append(compact[at])
        return both[0] + both[1]

    HALF = (pl.ds(0, 128), pl.ds(128, 128))
    sib_at, sib_here, sent = {}, set(), {}

    def to_sibling(order):
        for dz, dy in order:
            j = dz * 4 + dy
            for half in range(2):
                to_sib[j, HALF[half], :] = piece(dz, dy, 1, half)
            sib_at[j] = net.send(to_sib.at[j], from_sib.at[j], sib)

    def chip_sum(dz, dy, half):
        j = dz * 4 + dy
        if j not in sib_here:
            net.landed(sib_at[j], from_sib.at[j])
            sib_here.add(j)
        return piece(dz, dy, 0, half) + from_sib[j, HALF[half], :]

    def pass_on(name, buf, dz, dy, half, there, device, extra=()):
        total = chip_sum(dz, dy, half)
        for other_name, ref in extra:
            net.landed(sent[other_name, half], ref)
            total = total + ref[...]
        buf[HALF[half], :] = total
        sent[name, half] = net.send(buf.at[HALF[half]], there, device)

    def d2d_a():
        to_sibling(((1, 2), (1, 1), (1, 3)))

    def d2d_b():
        to_sibling(((0, 2), (1, 0), (0, 1), (0, 3), (0, 0)))

    def far_z(half):
        pass_on("z2", sum_z.at[0], 1, 2, half, r_z2.at[HALF[half]], zp)

    def far_y(half):
        pass_on("ya", sum_y.at[0], 1, 1, half, r_ya.at[HALF[half]], yp)
        pass_on("yb", sum_y.at[1], 1, 3, half, r_yb.at[HALF[half]], ym)

    def near_free():
        pass_on("p", sum_y.at[3], 0, 1, 1, r_p.at[HALF[1]], yp)
        pass_on("m", sum_y.at[4], 0, 3, 0, r_m.at[HALF[0]], ym)

    def middle(half):
        pass_on(
            "h", sum_y.at[2], 0, 2, half, r_h.at[half], (yp, ym)[half],
            (("z2", r_z2.at[HALF[half]]),),
        )

    def near_z(half):
        pass_on(
            "z0", sum_z.at[1], 1, 0, half, r_z0.at[HALF[half]], zp,
            (("ya", r_ya.at[HALF[half]]), ("yb", r_yb.at[HALF[half]])),
        )

    def near_p():
        pass_on("p", sum_y.at[3], 0, 1, 0, r_p.at[HALF[0]], yp, (("h", r_h.at[0]),))

    def near_m():
        pass_on("m", sum_y.at[4], 0, 3, 1, r_m.at[HALF[1]], ym, (("h", r_h.at[1]),))

    def last_own():
        for half in range(2):
            own_grad[HALF[half], :] += chip_sum(0, 0, half).astype(F32)

    def last():
        for half in range(2):
            total = own_grad[HALF[half], :]
            for name, ref in (("p", r_p), ("m", r_m), ("z0", r_z0)):
                net.landed(sent[name, half], ref.at[HALF[half]])
                total = total + ref[HALF[half], :].astype(F32)
            grad_events[HALF[half], :] = (
                upstream[HALF[half], :].astype(F32)
                + norm_back(total, hat_in[HALF[half], :], inv_in[HALF[half], :])
            ).astype(BF16)

    steps = dict(
        value_heads=value_heads, weight_v=weight_v, score_heads=score_heads, weight_k=weight_k,
        weight_q=weight_q, back_rows=back_rows, encode=encode, own_rows=own_rows, d2d_a=d2d_a,
        d2d_b=d2d_b, near_free=near_free, near_p=near_p, near_m=near_m, last_own=last_own,
        last=last,
    )
    for half in range(2):
        for step in (far_z, far_y, middle, near_z):
            steps[step.__name__ + str(half)] = functools.partial(step, half)
    for step in SCHEDULE:
        if step in parts:
            next(parts[step])
        else:
            steps[step]()
    net.drain()


def finish_kernel(gw, enc, gev, grad_in, grad_out, encoded, grad_events, full, sems):
    writes = [
        pltpu.make_async_copy(enc, encoded, sems.at[8]),
        pltpu.make_async_copy(gev, grad_events, sems.at[9]),
    ]
    for i in range(4):
        rows = pl.ds(i * 128, 128)
        full[rows, :] = gw[rows, :].astype(F32)
        writes += [
            pltpu.make_async_copy(full.at[rows, pl.ds(512, 2048)], grad_in.at[rows], sems.at[i]),
            pltpu.make_async_copy(full.at[rows, pl.ds(0, 512)], grad_out.at[rows], sems.at[4 + i]),
        ]
        for copy in writes[-2:]:
            copy.start()
    for copy in writes[:2]:
        copy.start()
    for copy in writes:
        copy.wait()


def finish(gw, enc, gev):
    hbm = pl.BlockSpec(memory_space=pl.ANY)
    vmem = pl.BlockSpec(memory_space=pltpu.VMEM)
    return pl.pallas_call(
        finish_kernel,
        out_shape=(
            jax.ShapeDtypeStruct((512, 2048), F32),
            jax.ShapeDtypeStruct((512, 512), F32),
            jax.ShapeDtypeStruct((256, D), BF16),
            jax.ShapeDtypeStruct((256, D), BF16),
        ),
        in_specs=[vmem] * 3,
        out_specs=(hbm,) * 4,
        scratch_shapes=[pltpu.VMEM((512, GCOLS), F32), pltpu.SemaphoreType.DMA((10,))],
        compiler_params=pltpu.CompilerParams(vmem_limit_bytes=24 * 2**20),
        name="finish",
    )(gw, enc, gev)


def local(events, upstream, lengths, block_slots, pattern, in_weight, out_weight):
    vmem = pl.BlockSpec(memory_space=pltpu.VMEM)
    smem = pl.BlockSpec(memory_space=pltpu.SMEM)
    hbm = pl.BlockSpec(memory_space=pl.ANY)
    v = pltpu.VMEM
    scratch = [
        v((512, 2048), BF16), v((512, 512), BF16), v((32, 128, 512), BF16),
        v((1024, 512), BF16), v((256, 512), BF16), v((256, 512), F32), v((256, 1), F32),
        v((4, 256, 128), BF16), v((4, 256, 128), F32),
        v((4, 256, 128), BF16), v((4, 256, 128), F32),
        v((4, 1024, 128), BF16), v((4, 1024, 128), F32),
        v((4, 1024, 128), BF16), v((4, 1024, 128), F32),
        v((4, 256, 128), F32), v((2, 128, 512), F32), v((8, 128, 512), BF16),
        v((8, 128, 512), F32), v((4, 256, 128), F32), v((4, 256, 128), BF16),
        v((4, 256, 128), F32),
        v((256, 512), BF16), v((256, 512), BF16), v((256, 512), BF16),
        v((4, 1024, 128), BF16), v((4, 1024, 128), BF16), v((256, 512), F32),
        v((7, 128, 512), BF16),
        v((8, 256, 512), BF16), v((8, 256, 512), BF16), v((5, 256, 512), BF16),
        v((2, 256, 512), BF16),
        v((256, 512), BF16), v((256, 512), BF16), v((256, 512), BF16), v((2, 128, 512), BF16),
        v((256, 512), BF16), v((256, 512), BF16), v((256, 512), BF16),
        v((512, GCOLS), BF16),
    ]
    for _, _, columns, _ in PARTS:
        half = columns // 2
        scratch += [
            v((512, half), BF16), v((4, 128, half), BF16), v((4, 32, half), BF16),
            v((4, 32, half), BF16), v((32, half), BF16),
        ]
    scratch += [
        pltpu.SemaphoreType.DMA((2,)),
        pltpu.SemaphoreType.DMA((N_SEM,)),
        pltpu.SemaphoreType.DMA((N_SEM,)),
    ]
    encoded, grad_events, gw = pl.pallas_call(
        layer_kernel,
        out_shape=(
            pltpu.VMEM((256, D), BF16),
            pltpu.VMEM((256, D), BF16),
            pltpu.VMEM((512, GCOLS), BF16),
        ),
        in_specs=[smem, smem, smem, vmem, vmem, hbm, hbm],
        out_specs=(vmem, vmem, vmem),
        scratch_shapes=scratch,
        compiler_params=pltpu.CompilerParams(
            collective_id=0, has_side_effects=True, vmem_limit_bytes=54 * 2**20
        ),
        name="layer",
    )(block_slots, pattern.T, lengths, events[0], upstream[0], in_weight, out_weight)
    grad_in, grad_out, encoded, grad_events = finish(gw, encoded, grad_events)
    return encoded[None], grad_events[None], grad_in, grad_out


def solution(mesh):
    return jax.shard_map(
        local,
        mesh=mesh,
        in_specs=(P("dp", "ctx", None), P("dp", "ctx", None), P("dp"), P(), P(), P(), P()),
        out_specs=(P("dp", "ctx", None), P("dp", "ctx", None), P(), P()),
        check_vma=False,
    )
```

```python
import functools

import jax
import jax.numpy as jnp
from jax import lax
from jax.experimental import pallas as pl
from jax.experimental.pallas import tpu as pltpu
from jax.sharding import PartitionSpec as P

HEADS = 4
HD = 128
BLK = 128
D = 512
EPS = 1e-05
SCALE = HD ** (-0.5)
MESH = pl.DeviceIdType.MESH
F32 = jnp.float32
BF16 = jnp.bfloat16
FAR = 1 << 20
G_OUT, G_U, G_V, G_Q, G_K = 0, 512, 1024, 1536, 2048
GCOLS = 2560
N_SEM = 176
PARTS = (
    ("a", G_OUT, 512, ("x", "y", "z")),
    ("b", G_U, 256, ("y", "z", "x")),
    ("c", G_U + 256, 256, ("z", "x", "y")),
    ("v", G_V, 512, ("z", "x", "y")),
    ("q", G_Q, 512, ("y", "z", "x")),
    ("k", G_K, 512, ("x", "y", "z")),
)
SCHEDULE = (
    "score_heads", "weight_k", "c", "weight_q", "q", "k", "a", "b", "value_heads",
    "weight_v", "c", "v", "k", "b", "v", "a", "q", "back_rows",
    "d2d_a", "c", "d2d_b", "own_rows", "b", "k", "far_z1", "far_y0", "v",
    "q", "a", "k", "far_z0", "c", "near_free", "v", "near_z0", "q",
    "a", "k", "middle1", "c", "b", "last_own", "far_y1", "encode", "q",
    "middle0", "v", "b", "c", "k", "a", "b", "v", "q",
    "c", "near_z1", "k", "a", "near_p", "c", "near_m", "b", "k",
    "b", "v", "q", "v", "a", "last", "q", "a",
)


def dot(a, b):
    return jnp.dot(a, b, preferred_element_type=F32)


def dot_nt(a, b):
    return lax.dot_general(a, b, (((1,), (1,)), ((), ())), preferred_element_type=F32)


def dot_tn(a, b):
    return lax.dot_general(a, b, (((0,), (0,)), ((), ())), preferred_element_type=F32)


def sigmoid(z):
    return 0.5 + 0.5 * jnp.tanh(0.5 * z)


def norm_rows(z):
    centre = z - jnp.mean(z, axis=-1, keepdims=True)
    inverse = lax.rsqrt(jnp.mean(centre * centre, axis=-1, keepdims=True) + EPS)
    return centre * inverse, inverse


def norm_back(grad, hat, inverse):
    return inverse * (
        grad
        - jnp.mean(grad, axis=-1, keepdims=True)
        - hat * jnp.mean(grad * hat, axis=-1, keepdims=True)
    )


class Net:
    def __init__(self, send_sems, recv_sems):
        self.send_sems, self.recv_sems = send_sems, recv_sems
        self.copies = []

    def send(self, src, dst, device):
        at = len(self.copies)
        copy = pltpu.make_async_remote_copy(
            src_ref=src,
            dst_ref=dst,
            send_sem=self.send_sems.at[at],
            recv_sem=self.recv_sems.at[at],
            device_id=device,
            device_id_type=MESH,
        )
        copy.start()
        self.copies.append((copy, device))
        return at

    def landed(self, at, ref):
        pltpu.make_async_remote_copy(
            src_ref=ref,
            dst_ref=ref,
            send_sem=self.send_sems.at[at],
            recv_sem=self.recv_sems.at[at],
            device_id=self.copies[at][1],
            device_id_type=MESH,
        ).wait_recv()

    def drain(self):
        for copy, _ in self.copies:
            copy.wait_send()


def layer_kernel(
    slots_ref, pattern_ref, length_ref, events_hbm, upstream_hbm, w_hbm, wo_hbm,
    encoded, grad_events, *rest,
):
    outs, rest = rest[: len(PARTS)], rest[len(PARTS) :]
    (
        w, wo, gx, normed, own_normed, hat_in, inv_in, u_act,
        u_slope, q_act, q_slope, k_act, k_slope, v_act, v_slope, grad_gated,
        limit_mask, weights, slope, mixed, grad_mixed, grad_q, gated, du,
        dq, dv, dk, own_grad, compact, to_sib, from_sib, sum_y,
        sum_z, r_z2, r_ya, r_yb, r_h, r_p, r_m, r_z0,
        events, upstream,
    ) = rest[:42]
    ar_bufs, (in_sems, send_sems, recv_sems) = rest[42:-3], rest[-3:]

    def part_bufs(i):
        return (ar_bufs[6 * i], outs[i], *ar_bufs[6 * i + 1 : 6 * i + 6])

    def store_columns(lo, values):
        for at in range(lo, lo + values.shape[1], 128):
            for i, (_, start, n, _) in enumerate(PARTS):
                if start <= at < start + n:
                    half = n // 2
                    c, off = (at - start) // half, (at - start) % half
                    part_bufs(i)[0][c, :, off : off + 128] = values[:, at - lo : at - lo + 128]

    dp = lax.axis_index("dp")
    ctx = lax.axis_index("ctx")
    x, zh = dp // 2, dp % 2
    zl, y, core = ctx // 8, (ctx // 2) % 4, ctx % 2
    z = zh * 2 + zl

    def dev(x, y, z, core):
        return {"dp": x * 2 + z // 2, "ctx": ((z % 2) * 4 + y) * 2 + core}

    def rot(v, by):
        return lax.rem(v + by, 4)

    sib = dev(x, y, z, 1 - core)
    yp, ym, y2 = (dev(x, rot(y, i), z, core) for i in (1, 3, 2))
    zp = dev(x, y, zh * 2 + 1 - zl, core)
    ring_x = [dev(rot(x, i), y, z, core) for i in range(4)]
    ring_y = [dev(x, rot(y, i), z, core) for i in range(4)]
    ring_z = [dev(x, y, rot(z, i), core) for i in range(4)]

    barrier = pltpu.get_barrier_semaphore()
    partners = [sib, yp, ym] + ring_z[1:] + [y2] + ring_x[1:]
    for partner in partners:
        pl.semaphore_signal(barrier, inc=1, device_id=partner, device_id_type=MESH)

    loads = [
        pltpu.make_async_copy(src, dst, in_sems.at[i])
        for i, (src, dst) in enumerate(
            ((events_hbm, events), (upstream_hbm, upstream), (w_hbm, w), (wo_hbm, wo))
        )
    ]
    for copy in loads:
        copy.start()
    loads[0].wait()

    net = Net(send_sems, recv_sems)

    def shard(dz, dy, side):
        zz = zl if dz == 0 else 1 - zl
        kk = core if side == 0 else 1 - core
        return ((zz * 4 + rot(y, dy)) * 2 + kk) * 2

    def rows(dz, dy, side=0, half=None):
        base = shard(dz, dy, side)
        if half is None:
            return gx.at[pl.ds(base, 2)]
        return gx.at[base + half]

    for half in range(2):
        gx[shard(0, 0, 0) + half] = events[half * 128 : half * 128 + 128, :]
    pl.semaphore_wait(barrier, len(partners))

    def forward(ref, device):
        return net.send(ref, ref, device)

    a_yp0 = forward(rows(0, 0, 0, 0), yp)
    a_ym0 = forward(rows(0, 0, 0, 1), ym)
    a_z0 = forward(rows(0, 0, 0, 0), zp)
    a_sib = forward(rows(0, 0), sib)
    a_yp1 = forward(rows(0, 0, 0, 1), yp)
    a_ym1 = forward(rows(0, 0, 0, 0), ym)
    a_z1 = forward(rows(0, 0, 0, 1), zp)

    hat, inv = norm_rows(events[...].astype(F32))
    hat_in[...] = hat
    inv_in[...] = inv
    own = hat.astype(BF16)
    own_normed[...] = own
    for b in range(2):
        normed[b * 512 : b * 512 + 128, :] = own[b * 128 : b * 128 + 128]
    for copy in loads[1:]:
        copy.wait()

    def activate(pre):
        sig = sigmoid(pre)
        act = pre * sig
        return act.astype(BF16), sig + act * (1.0 - sig)

    for h in range(4):
        act, sl = activate(dot(own_normed[...], w[:, h * 128 : h * 128 + 128]))
        u_act[h] = act
        u_slope[h] = sl
        act, sl = activate(dot(own_normed[...], w[:, 1024 + h * 128 : 1152 + h * 128]))
        q_act[h] = act
        q_slope[h] = sl

    net.landed(a_yp0, rows(0, 3, 0, 0))
    r_yp = forward(rows(0, 3, 0, 0), yp)
    net.landed(a_ym0, rows(0, 1, 0, 1))
    r_ym = forward(rows(0, 1, 0, 1), ym)
    net.landed(a_z0, rows(1, 0, 0, 0))
    f_yp0 = forward(rows(1, 0, 0, 0), yp)
    f_ym0 = forward(rows(1, 0, 0, 0), ym)

    for h in range(4):
        grad_gated[h] = dot_nt(upstream[...], wo[h * 128 : h * 128 + 128, :])

    def project(lo, n):
        for h in range(4):
            act, sl = activate(dot(normed[pl.ds(lo, n), :], w[:, 512 + h * 128 : 640 + h * 128]))
            v_act[h, pl.ds(lo, n), :] = act
            v_slope[h, pl.ds(lo, n), :] = sl
            act, sl = activate(dot(normed[pl.ds(lo, n), :], w[:, 1536 + h * 128 : 1664 + h * 128]))
            k_act[h, pl.ds(lo, n), :] = act
            k_slope[h, pl.ds(lo, n), :] = sl

    net.landed(a_yp1, rows(0, 3, 0, 1))
    d1 = forward(rows(0, 3), sib)
    net.landed(a_ym1, rows(0, 1, 0, 0))
    d2 = forward(rows(0, 1), sib)
    net.landed(a_z1, rows(1, 0, 0, 1))
    f_yp1 = forward(rows(1, 0, 0, 1), yp)
    f_ym1 = forward(rows(1, 0, 0, 1), ym)
    d3 = forward(rows(1, 0), sib)
    project(0, 128)
    project(512, 128)
    net.landed(r_yp, rows(0, 2, 0, 0))
    z2_0 = forward(rows(0, 2, 0, 0), zp)
    net.landed(r_ym, rows(0, 2, 0, 1))
    z2_1 = forward(rows(0, 2, 0, 1), zp)
    d4 = forward(rows(0, 2), sib)

    length = length_ref[0]
    listed, at_slot, fresh = [], [], []
    for b in range(2):
        mine = slots_ref[2 * ctx + b]
        picks = [mine] + [pattern_ref[t, mine] for t in range(3)]
        listed.append(picks)
        news = [None]
        for t in range(1, 4):
            new = picks[t] != picks[0]
            for s in range(1, t):
                new = jnp.logical_and(new, picks[t] != picks[s])
            news.append(new)
        fresh.append(news)
    found = [[jnp.int32(0)] * 4 for _ in range(2)]
    for s in range(32):
        block = slots_ref[s]
        for b in range(2):
            for t in range(1, 4):
                found[b][t] = jnp.where(block == listed[b][t], s, found[b][t])

    for b in range(2):
        q_pos = listed[b][0] * 128 + lax.broadcasted_iota(jnp.int32, (128, 128), 0)
        top = jnp.where(q_pos < length, q_pos, -1)
        lane = lax.broadcasted_iota(jnp.int32, (128, 128), 1)
        for t in range(4):
            start = listed[b][t] * 128
            if t:
                start = jnp.where(fresh[b][t], start, FAR)
            limit_mask[b, :, t * 128 : t * 128 + 128] = (start + lane <= top).astype(F32)

    net.landed(f_yp0, rows(1, 3, 0, 0))
    net.landed(f_yp1, rows(1, 3, 0, 1))
    d5 = forward(rows(1, 3), sib)
    net.landed(f_ym0, rows(1, 1, 0, 0))
    net.landed(f_ym1, rows(1, 1, 0, 1))
    d6 = forward(rows(1, 1), sib)
    net.landed(z2_0, rows(1, 2, 0, 0))
    d7 = forward(rows(1, 2, 0, 0), sib)
    net.landed(z2_1, rows(1, 2, 0, 1))
    d8 = forward(rows(1, 2, 0, 1), sib)
    for at, (dz, dy) in zip(
        (a_sib, d1, d2, d3, d4, d5, d6),
        ((0, 0), (0, 3), (0, 1), (1, 0), (0, 2), (1, 3), (1, 1)),
    ):
        net.landed(at, rows(dz, dy, 1))
    net.landed(d7, rows(1, 2, 1, 0))
    net.landed(d8, rows(1, 2, 1, 1))

    for b in range(2):
        for t in range(1, 4):
            block = gx[found[b][t]]
            normed[b * 512 + t * 128 : b * 512 + t * 128 + 128, :] = norm_rows(block.astype(F32))[
                0
            ].astype(BF16)
    project(128, 384)
    project(640, 384)

    def forward_head(i, carry):
        b, h = i // 4, i % 4
        q = q_act[h, pl.ds(pl.multiple_of(b * 128, 128), 128), :]
        s = dot_nt(q, k_act[h, pl.ds(pl.multiple_of(b * 512, 512), 512), :]) * SCALE
        mask = limit_mask[b]
        sig = sigmoid(s)
        act = s * sig
        weights[i] = (act * mask).astype(BF16)
        slope[i] = (sig + act * (1.0 - sig)) * (mask * SCALE)
        mixed[h, pl.ds(pl.multiple_of(b * 128, 128), 128), :] = dot(
            weights[i], v_act[h, pl.ds(pl.multiple_of(b * 512, 512), 512), :]
        )
        return carry

    lax.fori_loop(0, 8, forward_head, 0, unroll=8)

    def across(parts):
        return sum(jnp.sum(part, axis=-1, keepdims=True) for part in parts) * (1.0 / D)

    parts = [mixed[h] for h in range(4)]
    mean = across(parts)
    parts = [part - mean for part in parts]
    inv_mix = lax.rsqrt(across([part * part for part in parts]) + EPS)
    hats = [part * inv_mix for part in parts]
    us = [u_act[h].astype(F32) for h in range(4)]
    gated[...] = jnp.concatenate([(hats[h] * us[h]).astype(BF16) for h in range(4)], axis=1)
    ggs = [grad_gated[h] for h in range(4)]
    du[...] = jnp.concatenate(
        [(ggs[h] * hats[h] * u_slope[h]).astype(BF16) for h in range(4)], axis=1
    )
    ts = [ggs[h] * us[h] for h in range(4)]
    mean_t = across(ts)
    mean_th = across([ts[h] * hats[h] for h in range(4)])
    for h in range(4):
        grad_mixed[h] = (inv_mix * (ts[h] - mean_t - hats[h] * mean_th)).astype(BF16)
    store_columns(G_OUT, dot_tn(gated[...], upstream[...]).astype(BF16))
    store_columns(G_U, dot_tn(own_normed[...], du[...]).astype(BF16))

    place = {"x": x, "y": y, "z": z}
    rings = {"x": ring_x, "y": ring_y, "z": ring_z}

    def span(start, n):
        return pl.ds(pl.multiple_of(start, n), n)

    def add4(parts):
        return sum(part.astype(F32) for part in parts).astype(BF16)

    def reduce_columns(lo, n, axes, bufs):
        gp, gw, sibling, first, second, third, total = bufs
        a1, a2, a3 = axes
        p1, p2, p3 = (place[a] for a in axes)
        far_first, near_first = (2, 1, 3), (2, 3, 1)

        def rows1(p):
            return span(p * 128, 128)

        def rows2(p):
            return span(p1 * 128 + p * 32, 32)

        at = net.send(gp.at[1 - core], sibling, sib)
        yield
        net.landed(at, sibling)
        ats = []
        for i in far_first + (0,):
            block = rows1(rot(p1, i))
            sibling[block, :] = gp[core, block, :] + sibling[block, :]
            if i:
                ats.append(net.send(sibling.at[block], first.at[i], rings[a1][i]))
        yield
        for at, i in zip(ats, far_first):
            net.landed(at, first.at[i])
        first[0] = add4([sibling[rows1(p1), :], first[1], first[2], first[3]])
        ats = [
            net.send(first.at[0, span(rot(p2, i) * 32, 32)], second.at[i], rings[a2][i])
            for i in far_first
        ]
        yield
        for at, i in zip(ats, far_first):
            net.landed(at, second.at[i])
        total[...] = add4([first[0, span(p2 * 32, 32), :], second[1], second[2], second[3]])
        third[p3] = total[...]
        ats = [net.send(total, third.at[p3], rings[a3][i]) for i in far_first]
        yield
        for at, i in zip(ats, near_first):
            net.landed(at, third.at[rot(p3, i)])
        gw[core, rows2(p2), :] = add4([third[0], third[1], third[2], third[3]])
        here = gw.at[core, rows2(p2)]
        ats = [net.send(here, here, rings[a2][i]) for i in far_first]
        yield
        for at, i in zip(ats, near_first):
            net.landed(at, gw.at[core, rows2(rot(p2, i))])
        here = gw.at[core, rows1(p1)]
        ats = [net.send(here, here, rings[a1][i]) for i in far_first]
        back = [net.send(here, here, sib)]
        yield
        for at, i in zip(ats, near_first):
            there = gw.at[core, rows1(rot(p1, i))]
            net.landed(at, there)
            back.append(net.send(there, there, sib))
        yield
        for at, i in zip(back, (0,) + near_first):
            net.landed(at, gw.at[1 - core, rows1(rot(p1, i))])
        yield

    parts = {
        name: reduce_columns(lo, n, axes, part_bufs(i))
        for i, (name, lo, n, axes) in enumerate(PARTS)
    }

    def heads_of(ref):
        return jnp.concatenate([ref[h] for h in range(4)], axis=1)

    def value_head(i, carry):
        b, h = i // 4, i % 4
        k_rows = pl.ds(pl.multiple_of(b * 512, 512), 512)
        gm = grad_mixed[h, pl.ds(pl.multiple_of(b * 128, 128), 128), :]
        dv[h, k_rows, :] = (dot_tn(weights[i], gm) * v_slope[h, k_rows, :]).astype(BF16)
        return carry

    def value_heads():
        lax.fori_loop(0, 8, value_head, 0, unroll=8)

    def weight_v():
        store_columns(G_V, dot_tn(normed[...], heads_of(dv)).astype(BF16))

    def score_head(i, carry):
        b, h = i // 4, i % 4
        q_rows = pl.ds(pl.multiple_of(b * 128, 128), 128)
        k_rows = pl.ds(pl.multiple_of(b * 512, 512), 512)
        gm = grad_mixed[h, q_rows, :]
        q = q_act[h, q_rows, :]
        gs = (dot_nt(gm, v_act[h, k_rows, :]) * slope[i]).astype(BF16)
        grad_q[h, q_rows, :] = dot(gs, k_act[h, k_rows, :])
        dk[h, k_rows, :] = (dot_tn(gs, q) * k_slope[h, k_rows, :]).astype(BF16)
        return carry

    def score_heads():
        lax.fori_loop(0, 8, score_head, 0, unroll=8)

    def weight_k():
        store_columns(G_K, dot_tn(normed[...], heads_of(dk)).astype(BF16))

    def weight_q():
        dq[...] = jnp.concatenate(
            [(grad_q[h] * q_slope[h]).astype(BF16) for h in range(4)], axis=1
        )
        store_columns(G_Q, dot_tn(own_normed[...], dq[...]).astype(BF16))

    def back_rows():
        back = dot_nt(heads_of(dv), w[:, 512:1024]) + dot_nt(heads_of(dk), w[:, 1536:2048])
        for b in range(2):
            for t in range(1, 4):
                lo = b * 512 + t * 128
                compact[b * 3 + t - 1] = back[lo : lo + 128].astype(BF16)
            own_grad[b * 128 : b * 128 + 128, :] = back[b * 512 : b * 512 + 128]
        compact[6] = jnp.zeros((128, 512), BF16)

    def encode():
        encoded[...] = (events[...].astype(F32) + dot(gated[...], wo[...])).astype(BF16)

    def own_rows():
        own_grad[...] += dot_nt(du[...], w[:, 0:512]) + dot_nt(dq[...], w[:, 1024:1536])

    def piece(dz, dy, side, half):
        zz = zl if dz == 0 else 1 - zl
        kk = core if side == 0 else 1 - core
        slot = ((zz * 4 + rot(y, dy)) * 2 + kk) * 2 + half
        both = []
        for b in range(2):
            at = jnp.int32(6)
            for t in range(1, 4):
                hit = jnp.logical_and(found[b][t] == slot, fresh[b][t])
                at = jnp.where(hit, b * 3 + t - 1, at)
            both.append(compact[at])
        return both[0] + both[1]

    HALF = (pl.ds(0, 128), pl.ds(128, 128))
    sib_at, sib_here, sent = {}, set(), {}

    def to_sibling(order):
        for dz, dy in order:
            j = dz * 4 + dy
            for half in range(2):
                to_sib[j, HALF[half], :] = piece(dz, dy, 1, half)
            sib_at[j] = net.send(to_sib.at[j], from_sib.at[j], sib)

    def chip_sum(dz, dy, half):
        j = dz * 4 + dy
        if j not in sib_here:
            net.landed(sib_at[j], from_sib.at[j])
            sib_here.add(j)
        return piece(dz, dy, 0, half) + from_sib[j, HALF[half], :]

    def pass_on(name, buf, dz, dy, half, there, device, extra=()):
        total = chip_sum(dz, dy, half)
        for other_name, ref in extra:
            net.landed(sent[other_name, half], ref)
            total = total + ref[...]
        buf[HALF[half], :] = total
        sent[name, half] = net.send(buf.at[HALF[half]], there, device)

    def d2d_a():
        to_sibling(((1, 2), (1, 1), (1, 3)))

    def d2d_b():
        to_sibling(((0, 2), (1, 0), (0, 1), (0, 3), (0, 0)))

    def far_z(half):
        pass_on("z2", sum_z.at[0], 1, 2, half, r_z2.at[HALF[half]], zp)

    def far_y(half):
        pass_on("ya", sum_y.at[0], 1, 1, half, r_ya.at[HALF[half]], yp)
        pass_on("yb", sum_y.at[1], 1, 3, half, r_yb.at[HALF[half]], ym)

    def near_free():
        pass_on("p", sum_y.at[3], 0, 1, 1, r_p.at[HALF[1]], yp)
        pass_on("m", sum_y.at[4], 0, 3, 0, r_m.at[HALF[0]], ym)

    def middle(half):
        pass_on(
            "h", sum_y.at[2], 0, 2, half, r_h.at[half], (yp, ym)[half],
            (("z2", r_z2.at[HALF[half]]),),
        )

    def near_z(half):
        pass_on(
            "z0", sum_z.at[1], 1, 0, half, r_z0.at[HALF[half]], zp,
            (("ya", r_ya.at[HALF[half]]), ("yb", r_yb.at[HALF[half]])),
        )

    def near_p():
        pass_on("p", sum_y.at[3], 0, 1, 0, r_p.at[HALF[0]], yp, (("h", r_h.at[0]),))

    def near_m():
        pass_on("m", sum_y.at[4], 0, 3, 1, r_m.at[HALF[1]], ym, (("h", r_h.at[1]),))

    def last_own():
        for half in range(2):
            own_grad[HALF[half], :] += chip_sum(0, 0, half).astype(F32)

    def last():
        for half in range(2):
            total = own_grad[HALF[half], :]
            for name, ref in (("p", r_p), ("m", r_m), ("z0", r_z0)):
                net.landed(sent[name, half], ref.at[HALF[half]])
                total = total + ref[HALF[half], :].astype(F32)
            grad_events[HALF[half], :] = (
                upstream[HALF[half], :].astype(F32)
                + norm_back(total, hat_in[HALF[half], :], inv_in[HALF[half], :])
            ).astype(BF16)

    steps = dict(
        value_heads=value_heads, weight_v=weight_v, score_heads=score_heads, weight_k=weight_k,
        weight_q=weight_q, back_rows=back_rows, encode=encode, own_rows=own_rows, d2d_a=d2d_a,
        d2d_b=d2d_b, near_free=near_free, near_p=near_p, near_m=near_m, last_own=last_own,
        last=last,
    )
    for half in range(2):
        for step in (far_z, far_y, middle, near_z):
            steps[step.__name__ + str(half)] = functools.partial(step, half)
    for step in SCHEDULE:
        if step in parts:
            next(parts[step])
        else:
            steps[step]()
    net.drain()


def finish_kernel(enc, gev, *refs):
    gws, (grad_in, grad_out, encoded, grad_events, full, sems) = refs[:-6], refs[-6:]
    writes = [
        pltpu.make_async_copy(enc, encoded, sems.at[8]),
        pltpu.make_async_copy(gev, grad_events, sems.at[9]),
    ]
    for i in range(4):
        rows = pl.ds(i * 128, 128)
        for gw, (_, lo, n, _) in zip(gws, PARTS):
            half = n // 2
            for c in range(2):
                full[rows, lo + c * half : lo + c * half + half] = gw[c, rows, :].astype(F32)
        writes += [
            pltpu.make_async_copy(full.at[rows, pl.ds(512, 2048)], grad_in.at[rows], sems.at[i]),
            pltpu.make_async_copy(full.at[rows, pl.ds(0, 512)], grad_out.at[rows], sems.at[4 + i]),
        ]
        for copy in writes[-2:]:
            copy.start()
    for copy in writes[:2]:
        copy.start()
    for copy in writes:
        copy.wait()


def finish(gw, enc, gev):
    hbm = pl.BlockSpec(memory_space=pl.ANY)
    vmem = pl.BlockSpec(memory_space=pltpu.VMEM)
    return pl.pallas_call(
        finish_kernel,
        out_shape=(
            jax.ShapeDtypeStruct((512, 2048), F32),
            jax.ShapeDtypeStruct((512, 512), F32),
            jax.ShapeDtypeStruct((256, D), BF16),
            jax.ShapeDtypeStruct((256, D), BF16),
        ),
        in_specs=[vmem] * (2 + len(gw)),
        out_specs=(hbm,) * 4,
        scratch_shapes=[pltpu.VMEM((512, GCOLS), F32), pltpu.SemaphoreType.DMA((10,))],
        compiler_params=pltpu.CompilerParams(vmem_limit_bytes=24 * 2**20),
        name="finish",
    )(enc, gev, *gw)


def local(events, upstream, lengths, block_slots, pattern, in_weight, out_weight):
    vmem = pl.BlockSpec(memory_space=pltpu.VMEM)
    smem = pl.BlockSpec(memory_space=pltpu.SMEM)
    hbm = pl.BlockSpec(memory_space=pl.ANY)
    v = pltpu.VMEM
    scratch = [
        v((512, 2048), BF16), v((512, 512), BF16), v((32, 128, 512), BF16),
        v((1024, 512), BF16), v((256, 512), BF16), v((256, 512), F32), v((256, 1), F32),
        v((4, 256, 128), BF16), v((4, 256, 128), F32),
        v((4, 256, 128), BF16), v((4, 256, 128), F32),
        v((4, 1024, 128), BF16), v((4, 1024, 128), F32),
        v((4, 1024, 128), BF16), v((4, 1024, 128), F32),
        v((4, 256, 128), F32), v((2, 128, 512), F32), v((8, 128, 512), BF16),
        v((8, 128, 512), F32), v((4, 256, 128), F32), v((4, 256, 128), BF16),
        v((4, 256, 128), F32),
        v((256, 512), BF16), v((256, 512), BF16), v((256, 512), BF16),
        v((4, 1024, 128), BF16), v((4, 1024, 128), BF16), v((256, 512), F32),
        v((7, 128, 512), BF16),
        v((8, 256, 512), BF16), v((8, 256, 512), BF16), v((5, 256, 512), BF16),
        v((2, 256, 512), BF16),
        v((256, 512), BF16), v((256, 512), BF16), v((256, 512), BF16), v((2, 128, 512), BF16),
        v((256, 512), BF16), v((256, 512), BF16), v((256, 512), BF16),
        v((256, 512), BF16), v((256, 512), BF16),
    ]
    for _, _, columns, _ in PARTS:
        half = columns // 2
        scratch += [
            v((2, 512, half), BF16), v((512, half), BF16), v((4, 128, half), BF16), v((4, 32, half), BF16),
            v((4, 32, half), BF16), v((32, half), BF16),
        ]
    scratch += [
        pltpu.SemaphoreType.DMA((4,)),
        pltpu.SemaphoreType.DMA((N_SEM,)),
        pltpu.SemaphoreType.DMA((N_SEM,)),
    ]
    encoded, grad_events, *gw = pl.pallas_call(
        layer_kernel,
        out_shape=(
            pltpu.VMEM((256, D), BF16),
            pltpu.VMEM((256, D), BF16),
            *[pltpu.VMEM((2, 512, n // 2), BF16) for _, _, n, _ in PARTS],
        ),
        in_specs=[smem, smem, smem, hbm, hbm, hbm, hbm],
        out_specs=(vmem,) * (2 + len(PARTS)),
        scratch_shapes=scratch,
        compiler_params=pltpu.CompilerParams(
            collective_id=0, has_side_effects=True, vmem_limit_bytes=54 * 2**20
        ),
        name="layer",
    )(block_slots, pattern.T, lengths, events[0], upstream[0], in_weight, out_weight)
    grad_in, grad_out, encoded, grad_events = finish(gw, encoded, grad_events)
    return encoded[None], grad_events[None], grad_in, grad_out


def solution(mesh):
    return jax.shard_map(
        local,
        mesh=mesh,
        in_specs=(P("dp", "ctx", None), P("dp", "ctx", None), P("dp"), P(), P(), P(), P()),
        out_specs=(P("dp", "ctx", None), P("dp", "ctx", None), P(), P()),
        check_vma=False,
    )
```

```python
import functools

import jax
import jax.numpy as jnp
from jax import lax
from jax.experimental import pallas as pl
from jax.experimental.pallas import tpu as pltpu
from jax.sharding import PartitionSpec as P

HEADS = 4
HD = 128
BLK = 128
D = 512
EPS = 1e-05
SCALE = HD ** (-0.5)
MESH = pl.DeviceIdType.MESH
F32 = jnp.float32
BF16 = jnp.bfloat16
FAR = 1 << 20
G_OUT, G_U, G_V, G_Q, G_K = 0, 512, 1024, 1536, 2048
GCOLS = 2560
N_SEM = 176
PARTS = (
    ("a", G_OUT, 512, ("x", "y", "z")),
    ("b", G_U, 256, ("y", "z", "x")),
    ("c", G_U + 256, 256, ("z", "x", "y")),
    ("v", G_V, 512, ("z", "x", "y")),
    ("q", G_Q, 512, ("y", "z", "x")),
    ("k", G_K, 512, ("x", "y", "z")),
)
SCHEDULE = (
    "score_heads", "weight_k", "c", "weight_q", "q", "k", "a", "b", "value_heads",
    "weight_v", "c", "v", "k", "b", "v", "a", "q", "back_rows",
    "d2d_a", "c", "d2d_b", "own_rows", "b", "k", "far_z1", "far_y0", "v",
    "q", "a", "k", "far_z0", "c", "near_free", "v", "near_z0", "q",
    "a", "k", "middle1", "c", "b", "last_own", "far_y1", "encode", "q",
    "middle0", "v", "b", "c", "k", "a", "b", "v", "q",
    "c", "near_z1", "k", "a", "near_p", "c", "near_m", "b", "k",
    "b", "v", "q", "v", "a", "last", "q", "a",
)


def dot(a, b):
    return jnp.dot(a, b, preferred_element_type=F32)


def dot_nt(a, b):
    return lax.dot_general(a, b, (((1,), (1,)), ((), ())), preferred_element_type=F32)


def dot_tn(a, b):
    return lax.dot_general(a, b, (((0,), (0,)), ((), ())), preferred_element_type=F32)


def sigmoid(z):
    return 0.5 + 0.5 * jnp.tanh(0.5 * z)


def norm_rows(z):
    centre = z - jnp.mean(z, axis=-1, keepdims=True)
    inverse = lax.rsqrt(jnp.mean(centre * centre, axis=-1, keepdims=True) + EPS)
    return centre * inverse, inverse


def norm_back(grad, hat, inverse):
    return inverse * (
        grad
        - jnp.mean(grad, axis=-1, keepdims=True)
        - hat * jnp.mean(grad * hat, axis=-1, keepdims=True)
    )


class Net:
    def __init__(self, send_sems, recv_sems):
        self.send_sems, self.recv_sems = send_sems, recv_sems
        self.copies = []

    def send(self, src, dst, device):
        at = len(self.copies)
        copy = pltpu.make_async_remote_copy(
            src_ref=src,
            dst_ref=dst,
            send_sem=self.send_sems.at[at],
            recv_sem=self.recv_sems.at[at],
            device_id=device,
            device_id_type=MESH,
        )
        copy.start()
        self.copies.append((copy, device))
        return at

    def landed(self, at, ref):
        pltpu.make_async_remote_copy(
            src_ref=ref,
            dst_ref=ref,
            send_sem=self.send_sems.at[at],
            recv_sem=self.recv_sems.at[at],
            device_id=self.copies[at][1],
            device_id_type=MESH,
        ).wait_recv()

    def drain(self):
        for copy, _ in self.copies:
            copy.wait_send()


def layer_kernel(
    slots_ref, pattern_ref, length_ref, events_hbm, upstream_hbm, w_hbm, wo_hbm,
    encoded, grad_events, *rest,
):
    outs, rest = rest[: len(PARTS)], rest[len(PARTS) :]
    (
        w, wo, gx, normed, own_normed, hat_in, inv_in, u_act,
        u_slope, q_act, q_slope, k_act, k_slope, v_act, v_slope, grad_gated,
        limit_mask, weights, slope, mixed, grad_mixed, grad_q, gated, du,
        dq, dv, dk, own_grad, compact, to_sib, from_sib, sum_y,
        sum_z, r_z2, r_ya, r_yb, r_h, r_p, r_m, r_z0,
        events, upstream,
    ) = rest[:42]
    ar_bufs, (in_sems, send_sems, recv_sems) = rest[42:-3], rest[-3:]

    def part_bufs(i):
        return (ar_bufs[6 * i], outs[i], *ar_bufs[6 * i + 1 : 6 * i + 6])

    def store_columns(lo, values):
        for at in range(lo, lo + values.shape[1], 128):
            for i, (_, start, n, _) in enumerate(PARTS):
                if start <= at < start + n:
                    half = n // 2
                    c, off = (at - start) // half, (at - start) % half
                    part_bufs(i)[0][c, :, off : off + 128] = values[:, at - lo : at - lo + 128]

    dp = lax.axis_index("dp")
    ctx = lax.axis_index("ctx")
    x, zh = dp // 2, dp % 2
    zl, y, core = ctx // 8, (ctx // 2) % 4, ctx % 2
    z = zh * 2 + zl

    def dev(x, y, z, core):
        return {"dp": x * 2 + z // 2, "ctx": ((z % 2) * 4 + y) * 2 + core}

    def rot(v, by):
        return lax.rem(v + by, 4)

    sib = dev(x, y, z, 1 - core)
    yp, ym, y2 = (dev(x, rot(y, i), z, core) for i in (1, 3, 2))
    zp = dev(x, y, zh * 2 + 1 - zl, core)
    ring_x = [dev(rot(x, i), y, z, core) for i in range(4)]
    ring_y = [dev(x, rot(y, i), z, core) for i in range(4)]
    ring_z = [dev(x, y, rot(z, i), core) for i in range(4)]

    barrier = pltpu.get_barrier_semaphore()
    partners = [sib, yp, ym] + ring_z[1:] + [y2] + ring_x[1:]
    for partner in partners:
        pl.semaphore_signal(barrier, inc=1, device_id=partner, device_id_type=MESH)

    loads = [
        pltpu.make_async_copy(src, dst, in_sems.at[i])
        for i, (src, dst) in enumerate(
            ((events_hbm, events), (upstream_hbm, upstream), (w_hbm, w), (wo_hbm, wo))
        )
    ]

    net = Net(send_sems, recv_sems)

    def shard(dz, dy, side):
        zz = zl if dz == 0 else 1 - zl
        kk = core if side == 0 else 1 - core
        return ((zz * 4 + rot(y, dy)) * 2 + kk) * 2

    def rows(dz, dy, side=0, half=None):
        base = shard(dz, dy, side)
        if half is None:
            return gx.at[pl.ds(base, 2)]
        return gx.at[base + half]

    first_rows = [
        pltpu.make_async_copy(
            events_hbm.at[pl.ds(half * 128, 128)],
            gx.at[shard(0, 0, 0) + half],
            in_sems.at[4 + half],
        )
        for half in range(2)
    ]
    for copy in first_rows + loads:
        copy.start()
    for copy in first_rows:
        copy.wait()
    pl.semaphore_wait(barrier, len(partners))

    def forward(ref, device):
        return net.send(ref, ref, device)

    a_yp0 = forward(rows(0, 0, 0, 0), yp)
    a_ym0 = forward(rows(0, 0, 0, 1), ym)
    a_z0 = forward(rows(0, 0, 0, 0), zp)
    a_sib = forward(rows(0, 0), sib)
    a_yp1 = forward(rows(0, 0, 0, 1), yp)
    a_ym1 = forward(rows(0, 0, 0, 0), ym)
    a_z1 = forward(rows(0, 0, 0, 1), zp)

    for copy in loads:
        copy.wait()
    hat, inv = norm_rows(events[...].astype(F32))
    hat_in[...] = hat
    inv_in[...] = inv
    own = hat.astype(BF16)
    own_normed[...] = own
    for b in range(2):
        normed[b * 512 : b * 512 + 128, :] = own[b * 128 : b * 128 + 128]

    def activate(pre):
        sig = sigmoid(pre)
        act = pre * sig
        return act.astype(BF16), sig + act * (1.0 - sig)

    for h in range(4):
        act, sl = activate(dot(own_normed[...], w[:, h * 128 : h * 128 + 128]))
        u_act[h] = act
        u_slope[h] = sl
        act, sl = activate(dot(own_normed[...], w[:, 1024 + h * 128 : 1152 + h * 128]))
        q_act[h] = act
        q_slope[h] = sl

    net.landed(a_yp0, rows(0, 3, 0, 0))
    r_yp = forward(rows(0, 3, 0, 0), yp)
    net.landed(a_ym0, rows(0, 1, 0, 1))
    r_ym = forward(rows(0, 1, 0, 1), ym)
    net.landed(a_z0, rows(1, 0, 0, 0))
    f_yp0 = forward(rows(1, 0, 0, 0), yp)
    f_ym0 = forward(rows(1, 0, 0, 0), ym)

    for h in range(4):
        grad_gated[h] = dot_nt(upstream[...], wo[h * 128 : h * 128 + 128, :])

    def project(lo, n):
        for h in range(4):
            act, sl = activate(dot(normed[pl.ds(lo, n), :], w[:, 512 + h * 128 : 640 + h * 128]))
            v_act[h, pl.ds(lo, n), :] = act
            v_slope[h, pl.ds(lo, n), :] = sl
            act, sl = activate(dot(normed[pl.ds(lo, n), :], w[:, 1536 + h * 128 : 1664 + h * 128]))
            k_act[h, pl.ds(lo, n), :] = act
            k_slope[h, pl.ds(lo, n), :] = sl

    net.landed(a_yp1, rows(0, 3, 0, 1))
    d1 = forward(rows(0, 3), sib)
    net.landed(a_ym1, rows(0, 1, 0, 0))
    d2 = forward(rows(0, 1), sib)
    net.landed(a_z1, rows(1, 0, 0, 1))
    f_yp1 = forward(rows(1, 0, 0, 1), yp)
    f_ym1 = forward(rows(1, 0, 0, 1), ym)
    d3 = forward(rows(1, 0), sib)
    project(0, 128)
    project(512, 128)
    net.landed(r_yp, rows(0, 2, 0, 0))
    z2_0 = forward(rows(0, 2, 0, 0), zp)
    net.landed(r_ym, rows(0, 2, 0, 1))
    z2_1 = forward(rows(0, 2, 0, 1), zp)
    d4 = forward(rows(0, 2), sib)

    length = length_ref[0]
    listed, at_slot, fresh = [], [], []
    for b in range(2):
        mine = slots_ref[2 * ctx + b]
        picks = [mine] + [pattern_ref[t, mine] for t in range(3)]
        listed.append(picks)
        news = [None]
        for t in range(1, 4):
            new = picks[t] != picks[0]
            for s in range(1, t):
                new = jnp.logical_and(new, picks[t] != picks[s])
            news.append(new)
        fresh.append(news)
    found = [[jnp.int32(0)] * 4 for _ in range(2)]
    for s in range(32):
        block = slots_ref[s]
        for b in range(2):
            for t in range(1, 4):
                found[b][t] = jnp.where(block == listed[b][t], s, found[b][t])

    for b in range(2):
        q_pos = listed[b][0] * 128 + lax.broadcasted_iota(jnp.int32, (128, 128), 0)
        top = jnp.where(q_pos < length, q_pos, -1)
        lane = lax.broadcasted_iota(jnp.int32, (128, 128), 1)
        for t in range(4):
            start = listed[b][t] * 128
            if t:
                start = jnp.where(fresh[b][t], start, FAR)
            limit_mask[b, :, t * 128 : t * 128 + 128] = (start + lane <= top).astype(F32)

    net.landed(f_yp0, rows(1, 3, 0, 0))
    net.landed(f_yp1, rows(1, 3, 0, 1))
    d5 = forward(rows(1, 3), sib)
    net.landed(f_ym0, rows(1, 1, 0, 0))
    net.landed(f_ym1, rows(1, 1, 0, 1))
    d6 = forward(rows(1, 1), sib)
    net.landed(z2_0, rows(1, 2, 0, 0))
    d7 = forward(rows(1, 2, 0, 0), sib)
    net.landed(z2_1, rows(1, 2, 0, 1))
    d8 = forward(rows(1, 2, 0, 1), sib)
    for at, (dz, dy) in zip(
        (a_sib, d1, d2, d3, d4, d5, d6),
        ((0, 0), (0, 3), (0, 1), (1, 0), (0, 2), (1, 3), (1, 1)),
    ):
        net.landed(at, rows(dz, dy, 1))
    net.landed(d7, rows(1, 2, 1, 0))
    net.landed(d8, rows(1, 2, 1, 1))

    for b in range(2):
        for t in range(1, 4):
            block = gx[found[b][t]]
            normed[b * 512 + t * 128 : b * 512 + t * 128 + 128, :] = norm_rows(block.astype(F32))[
                0
            ].astype(BF16)
    project(128, 384)
    project(640, 384)

    def forward_head(i, carry):
        b, h = i // 4, i % 4
        q = q_act[h, pl.ds(pl.multiple_of(b * 128, 128), 128), :]
        s = dot_nt(q, k_act[h, pl.ds(pl.multiple_of(b * 512, 512), 512), :]) * SCALE
        mask = limit_mask[b]
        sig = sigmoid(s)
        act = s * sig
        weights[i] = (act * mask).astype(BF16)
        slope[i] = (sig + act * (1.0 - sig)) * (mask * SCALE)
        mixed[h, pl.ds(pl.multiple_of(b * 128, 128), 128), :] = dot(
            weights[i], v_act[h, pl.ds(pl.multiple_of(b * 512, 512), 512), :]
        )
        return carry

    lax.fori_loop(0, 8, forward_head, 0, unroll=8)

    def across(parts):
        return sum(jnp.sum(part, axis=-1, keepdims=True) for part in parts) * (1.0 / D)

    parts = [mixed[h] for h in range(4)]
    mean = across(parts)
    parts = [part - mean for part in parts]
    inv_mix = lax.rsqrt(across([part * part for part in parts]) + EPS)
    hats = [part * inv_mix for part in parts]
    us = [u_act[h].astype(F32) for h in range(4)]
    gated[...] = jnp.concatenate([(hats[h] * us[h]).astype(BF16) for h in range(4)], axis=1)
    ggs = [grad_gated[h] for h in range(4)]
    du[...] = jnp.concatenate(
        [(ggs[h] * hats[h] * u_slope[h]).astype(BF16) for h in range(4)], axis=1
    )
    ts = [ggs[h] * us[h] for h in range(4)]
    mean_t = across(ts)
    mean_th = across([ts[h] * hats[h] for h in range(4)])
    for h in range(4):
        grad_mixed[h] = (inv_mix * (ts[h] - mean_t - hats[h] * mean_th)).astype(BF16)
    store_columns(G_OUT, dot_tn(gated[...], upstream[...]).astype(BF16))
    store_columns(G_U, dot_tn(own_normed[...], du[...]).astype(BF16))

    place = {"x": x, "y": y, "z": z}
    rings = {"x": ring_x, "y": ring_y, "z": ring_z}

    def span(start, n):
        return pl.ds(pl.multiple_of(start, n), n)

    def add4(parts):
        return sum(part.astype(F32) for part in parts).astype(BF16)

    def reduce_columns(lo, n, axes, bufs):
        gp, gw, sibling, first, second, third, total = bufs
        a1, a2, a3 = axes
        p1, p2, p3 = (place[a] for a in axes)
        far_first, near_first = (2, 1, 3), (2, 3, 1)

        def rows1(p):
            return span(p * 128, 128)

        def rows2(p):
            return span(p1 * 128 + p * 32, 32)

        at = net.send(gp.at[1 - core], sibling, sib)
        yield
        net.landed(at, sibling)
        ats = []
        for i in far_first + (0,):
            block = rows1(rot(p1, i))
            sibling[block, :] = gp[core, block, :] + sibling[block, :]
            if i:
                ats.append(net.send(sibling.at[block], first.at[i], rings[a1][i]))
        yield
        for at, i in zip(ats, far_first):
            net.landed(at, first.at[i])
        first[0] = add4([sibling[rows1(p1), :], first[1], first[2], first[3]])
        ats = [
            net.send(first.at[0, span(rot(p2, i) * 32, 32)], second.at[i], rings[a2][i])
            for i in far_first
        ]
        yield
        for at, i in zip(ats, far_first):
            net.landed(at, second.at[i])
        total[...] = add4([first[0, span(p2 * 32, 32), :], second[1], second[2], second[3]])
        third[p3] = total[...]
        ats = [net.send(total, third.at[p3], rings[a3][i]) for i in far_first]
        yield
        for at, i in zip(ats, near_first):
            net.landed(at, third.at[rot(p3, i)])
        gw[core, rows2(p2), :] = add4([third[0], third[1], third[2], third[3]])
        here = gw.at[core, rows2(p2)]
        ats = [net.send(here, here, rings[a2][i]) for i in far_first]
        yield
        for at, i in zip(ats, near_first):
            net.landed(at, gw.at[core, rows2(rot(p2, i))])
        here = gw.at[core, rows1(p1)]
        ats = [net.send(here, here, rings[a1][i]) for i in far_first]
        back = [net.send(here, here, sib)]
        yield
        for at, i in zip(ats, near_first):
            there = gw.at[core, rows1(rot(p1, i))]
            net.landed(at, there)
            back.append(net.send(there, there, sib))
        yield
        for at, i in zip(back, (0,) + near_first):
            net.landed(at, gw.at[1 - core, rows1(rot(p1, i))])
        yield

    parts = {
        name: reduce_columns(lo, n, axes, part_bufs(i))
        for i, (name, lo, n, axes) in enumerate(PARTS)
    }

    def heads_of(ref):
        return jnp.concatenate([ref[h] for h in range(4)], axis=1)

    def value_head(i, carry):
        b, h = i // 4, i % 4
        k_rows = pl.ds(pl.multiple_of(b * 512, 512), 512)
        gm = grad_mixed[h, pl.ds(pl.multiple_of(b * 128, 128), 128), :]
        dv[h, k_rows, :] = (dot_tn(weights[i], gm) * v_slope[h, k_rows, :]).astype(BF16)
        return carry

    def value_heads():
        lax.fori_loop(0, 8, value_head, 0, unroll=8)

    def weight_v():
        store_columns(G_V, dot_tn(normed[...], heads_of(dv)).astype(BF16))

    def score_head(i, carry):
        b, h = i // 4, i % 4
        q_rows = pl.ds(pl.multiple_of(b * 128, 128), 128)
        k_rows = pl.ds(pl.multiple_of(b * 512, 512), 512)
        gm = grad_mixed[h, q_rows, :]
        q = q_act[h, q_rows, :]
        gs = (dot_nt(gm, v_act[h, k_rows, :]) * slope[i]).astype(BF16)
        grad_q[h, q_rows, :] = dot(gs, k_act[h, k_rows, :])
        dk[h, k_rows, :] = (dot_tn(gs, q) * k_slope[h, k_rows, :]).astype(BF16)
        return carry

    def score_heads():
        lax.fori_loop(0, 8, score_head, 0, unroll=8)

    def weight_k():
        store_columns(G_K, dot_tn(normed[...], heads_of(dk)).astype(BF16))

    def weight_q():
        dq[...] = jnp.concatenate(
            [(grad_q[h] * q_slope[h]).astype(BF16) for h in range(4)], axis=1
        )
        store_columns(G_Q, dot_tn(own_normed[...], dq[...]).astype(BF16))

    def back_rows():
        back = dot_nt(heads_of(dv), w[:, 512:1024]) + dot_nt(heads_of(dk), w[:, 1536:2048])
        for b in range(2):
            for t in range(1, 4):
                lo = b * 512 + t * 128
                compact[b * 3 + t - 1] = back[lo : lo + 128].astype(BF16)
            own_grad[b * 128 : b * 128 + 128, :] = back[b * 512 : b * 512 + 128]
        compact[6] = jnp.zeros((128, 512), BF16)

    def encode():
        encoded[...] = (events[...].astype(F32) + dot(gated[...], wo[...])).astype(BF16)

    def own_rows():
        own_grad[...] += dot_nt(du[...], w[:, 0:512]) + dot_nt(dq[...], w[:, 1024:1536])

    def piece(dz, dy, side, half):
        zz = zl if dz == 0 else 1 - zl
        kk = core if side == 0 else 1 - core
        slot = ((zz * 4 + rot(y, dy)) * 2 + kk) * 2 + half
        both = []
        for b in range(2):
            at = jnp.int32(6)
            for t in range(1, 4):
                hit = jnp.logical_and(found[b][t] == slot, fresh[b][t])
                at = jnp.where(hit, b * 3 + t - 1, at)
            both.append(compact[at])
        return both[0] + both[1]

    HALF = (pl.ds(0, 128), pl.ds(128, 128))
    sib_at, sib_here, sent = {}, set(), {}

    def to_sibling(order):
        for dz, dy in order:
            j = dz * 4 + dy
            for half in range(2):
                to_sib[j, HALF[half], :] = piece(dz, dy, 1, half)
            sib_at[j] = net.send(to_sib.at[j], from_sib.at[j], sib)

    def chip_sum(dz, dy, half):
        j = dz * 4 + dy
        if j not in sib_here:
            net.landed(sib_at[j], from_sib.at[j])
            sib_here.add(j)
        return piece(dz, dy, 0, half) + from_sib[j, HALF[half], :]

    def pass_on(name, buf, dz, dy, half, there, device, extra=()):
        total = chip_sum(dz, dy, half)
        for other_name, ref in extra:
            net.landed(sent[other_name, half], ref)
            total = total + ref[...]
        buf[HALF[half], :] = total
        sent[name, half] = net.send(buf.at[HALF[half]], there, device)

    def d2d_a():
        to_sibling(((1, 2), (1, 1), (1, 3)))

    def d2d_b():
        to_sibling(((0, 2), (1, 0), (0, 1), (0, 3), (0, 0)))

    def far_z(half):
        pass_on("z2", sum_z.at[0], 1, 2, half, r_z2.at[HALF[half]], zp)

    def far_y(half):
        pass_on("ya", sum_y.at[0], 1, 1, half, r_ya.at[HALF[half]], yp)
        pass_on("yb", sum_y.at[1], 1, 3, half, r_yb.at[HALF[half]], ym)

    def near_free():
        pass_on("p", sum_y.at[3], 0, 1, 1, r_p.at[HALF[1]], yp)
        pass_on("m", sum_y.at[4], 0, 3, 0, r_m.at[HALF[0]], ym)

    def middle(half):
        pass_on(
            "h", sum_y.at[2], 0, 2, half, r_h.at[half], (yp, ym)[half],
            (("z2", r_z2.at[HALF[half]]),),
        )

    def near_z(half):
        pass_on(
            "z0", sum_z.at[1], 1, 0, half, r_z0.at[HALF[half]], zp,
            (("ya", r_ya.at[HALF[half]]), ("yb", r_yb.at[HALF[half]])),
        )

    def near_p():
        pass_on("p", sum_y.at[3], 0, 1, 0, r_p.at[HALF[0]], yp, (("h", r_h.at[0]),))

    def near_m():
        pass_on("m", sum_y.at[4], 0, 3, 1, r_m.at[HALF[1]], ym, (("h", r_h.at[1]),))

    def last_own():
        for half in range(2):
            own_grad[HALF[half], :] += chip_sum(0, 0, half).astype(F32)

    def last():
        for half in range(2):
            total = own_grad[HALF[half], :]
            for name, ref in (("p", r_p), ("m", r_m), ("z0", r_z0)):
                net.landed(sent[name, half], ref.at[HALF[half]])
                total = total + ref[HALF[half], :].astype(F32)
            grad_events[HALF[half], :] = (
                upstream[HALF[half], :].astype(F32)
                + norm_back(total, hat_in[HALF[half], :], inv_in[HALF[half], :])
            ).astype(BF16)

    steps = dict(
        value_heads=value_heads, weight_v=weight_v, score_heads=score_heads, weight_k=weight_k,
        weight_q=weight_q, back_rows=back_rows, encode=encode, own_rows=own_rows, d2d_a=d2d_a,
        d2d_b=d2d_b, near_free=near_free, near_p=near_p, near_m=near_m, last_own=last_own,
        last=last,
    )
    for half in range(2):
        for step in (far_z, far_y, middle, near_z):
            steps[step.__name__ + str(half)] = functools.partial(step, half)
    for step in SCHEDULE:
        if step in parts:
            next(parts[step])
        else:
            steps[step]()
    net.drain()


def finish_kernel(enc, gev, *refs):
    gws, (grad_in, grad_out, encoded, grad_events, full, sems) = refs[:-6], refs[-6:]
    writes = [
        pltpu.make_async_copy(enc, encoded, sems.at[8]),
        pltpu.make_async_copy(gev, grad_events, sems.at[9]),
    ]
    for i in range(4):
        rows = pl.ds(i * 128, 128)
        for gw, (_, lo, n, _) in zip(gws, PARTS):
            half = n // 2
            for c in range(2):
                full[rows, lo + c * half : lo + c * half + half] = gw[c, rows, :].astype(F32)
        writes += [
            pltpu.make_async_copy(full.at[rows, pl.ds(512, 2048)], grad_in.at[rows], sems.at[i]),
            pltpu.make_async_copy(full.at[rows, pl.ds(0, 512)], grad_out.at[rows], sems.at[4 + i]),
        ]
        for copy in writes[-2:]:
            copy.start()
    for copy in writes[:2]:
        copy.start()
    for copy in writes:
        copy.wait()


def finish(gw, enc, gev):
    hbm = pl.BlockSpec(memory_space=pl.ANY)
    vmem = pl.BlockSpec(memory_space=pltpu.VMEM)
    return pl.pallas_call(
        finish_kernel,
        out_shape=(
            jax.ShapeDtypeStruct((512, 2048), F32),
            jax.ShapeDtypeStruct((512, 512), F32),
            jax.ShapeDtypeStruct((256, D), BF16),
            jax.ShapeDtypeStruct((256, D), BF16),
        ),
        in_specs=[vmem] * (2 + len(gw)),
        out_specs=(hbm,) * 4,
        scratch_shapes=[pltpu.VMEM((512, GCOLS), F32), pltpu.SemaphoreType.DMA((10,))],
        compiler_params=pltpu.CompilerParams(vmem_limit_bytes=24 * 2**20),
        name="finish",
    )(enc, gev, *gw)


def local(events, upstream, lengths, block_slots, pattern, in_weight, out_weight):
    vmem = pl.BlockSpec(memory_space=pltpu.VMEM)
    smem = pl.BlockSpec(memory_space=pltpu.SMEM)
    hbm = pl.BlockSpec(memory_space=pl.ANY)
    v = pltpu.VMEM
    scratch = [
        v((512, 2048), BF16), v((512, 512), BF16), v((32, 128, 512), BF16),
        v((1024, 512), BF16), v((256, 512), BF16), v((256, 512), F32), v((256, 1), F32),
        v((4, 256, 128), BF16), v((4, 256, 128), F32),
        v((4, 256, 128), BF16), v((4, 256, 128), F32),
        v((4, 1024, 128), BF16), v((4, 1024, 128), F32),
        v((4, 1024, 128), BF16), v((4, 1024, 128), F32),
        v((4, 256, 128), F32), v((2, 128, 512), F32), v((8, 128, 512), BF16),
        v((8, 128, 512), F32), v((4, 256, 128), F32), v((4, 256, 128), BF16),
        v((4, 256, 128), F32),
        v((256, 512), BF16), v((256, 512), BF16), v((256, 512), BF16),
        v((4, 1024, 128), BF16), v((4, 1024, 128), BF16), v((256, 512), F32),
        v((7, 128, 512), BF16),
        v((8, 256, 512), BF16), v((8, 256, 512), BF16), v((5, 256, 512), BF16),
        v((2, 256, 512), BF16),
        v((256, 512), BF16), v((256, 512), BF16), v((256, 512), BF16), v((2, 128, 512), BF16),
        v((256, 512), BF16), v((256, 512), BF16), v((256, 512), BF16),
        v((256, 512), BF16), v((256, 512), BF16),
    ]
    for _, _, columns, _ in PARTS:
        half = columns // 2
        scratch += [
            v((2, 512, half), BF16), v((512, half), BF16), v((4, 128, half), BF16), v((4, 32, half), BF16),
            v((4, 32, half), BF16), v((32, half), BF16),
        ]
    scratch += [
        pltpu.SemaphoreType.DMA((6,)),
        pltpu.SemaphoreType.DMA((N_SEM,)),
        pltpu.SemaphoreType.DMA((N_SEM,)),
    ]
    encoded, grad_events, *gw = pl.pallas_call(
        layer_kernel,
        out_shape=(
            pltpu.VMEM((256, D), BF16),
            pltpu.VMEM((256, D), BF16),
            *[pltpu.VMEM((2, 512, n // 2), BF16) for _, _, n, _ in PARTS],
        ),
        in_specs=[smem, smem, smem, hbm, hbm, hbm, hbm],
        out_specs=(vmem,) * (2 + len(PARTS)),
        scratch_shapes=scratch,
        compiler_params=pltpu.CompilerParams(
            collective_id=0, has_side_effects=True, vmem_limit_bytes=54 * 2**20
        ),
        name="layer",
    )(block_slots, pattern.T, lengths, events[0], upstream[0], in_weight, out_weight)
    grad_in, grad_out, encoded, grad_events = finish(gw, encoded, grad_events)
    return encoded[None], grad_events[None], grad_in, grad_out


def solution(mesh):
    return jax.shard_map(
        local,
        mesh=mesh,
        in_specs=(P("dp", "ctx", None), P("dp", "ctx", None), P("dp"), P(), P(), P(), P()),
        out_specs=(P("dp", "ctx", None), P("dp", "ctx", None), P(), P()),
        check_vma=False,
    )
```
